256 devices in a mesh: seq: 64 (over y, z, core), dp: 4 (over x).
Axes of the slice: x: 4, y: 4, z: 8, core: 2. Of those that a mesh axis runs over, the one named last changes fastest.
Arguments:
- streams: bfloat16 [4, 8192, 3, 4096], P('dp', 'seq'), may hold values from -6 to 6
- cotangent: bfloat16 [4, 8192, 4096], P('dp', 'seq'), may hold values from -6 to 6
- doc_ids: int32 [4, 8192], P('dp', 'seq'), may hold values from 0 to 63, never falling along the last dimension, each value on 1 to 512 neighbouring positions
- short_taps: float32 [3, 3, 4096], P(None, None, 'seq'), may hold values from -3.5 to 3.5
- long_taps: float32 [256, 128], P('seq'), may hold values from -0.5 to 0.5
- skip_gain: float32 [4096], P('seq'), may hold values from 0.5 to 1.5
Outputs:
- mixed_out: bfloat16 [4, 8192, 4096], P('dp', 'seq')
- stream_grad: bfloat16 [4, 8192, 3, 4096], P('dp', 'seq')
- short_grad: float32 [3, 3, 4096], P(None, None, 'seq')
- taps_grad: float32 [256, 128], P('seq')
- gain_grad: float32 [4096], P('seq')
The draws below stay inside these ranges and needn't reach their ends.
Inputs may be any that keep to these rules, and one draw needn't show every extreme that they name: `doc_ids`: along each packed sequence the ids start at 0, never fall and rise by one at each document start; each document has 1 to 512 tokens, and one has exactly 512.
All inputs are finite; a program needn't handle non-finite values.
Results may differ from the reference program's by a relative error of at most 0.005.
Values may be sent and summed in bfloat16 or wider, within the bound.
A program may use at most 256 MiB of HBM per device.

```python
import math
import jax
import jax.numpy as jnp
import numpy as np
from jax import lax

D = 4096
SHORT = 3
LTAPS = 128
TOKENS = 8192
SEQS = 4
GROUPS = 256
DOCS = 64
DOC_MOST = 512


def steps_of(own_key, dims, split, least, largest):
    level, own = 1.0, jax.random.fold_in(own_key, 6)
    for position, parts in split:
        heights = jnp.exp(jax.random.uniform(jax.random.fold_in(own, position), (parts,), jnp.float32, least / len(split), largest / len(split)))
        level = level * jnp.repeat(heights, dims[position] // parts).reshape([-1 if axis == position else 1 for axis in range(len(dims))])
    return level


def profile(count, total, bound, skew):
    loads = [(1 << 20) // math.isqrt(grade ** skew) + 1 for grade in range(2, count + 1)]
    surplus, holding = total - bound - (count - 1), [1] * (count - 1)
    while surplus > 0:
        free = [i for i in range(count - 1) if holding[i] < bound]
        whole, remaining = sum([loads[i] for i in free]), surplus
        for i in free:
            addition = min(bound - holding[i], max(1, remaining * loads[i] // whole), surplus)
            holding[i] = holding[i] + addition
            surplus = surplus - addition
    return np.array([bound] + holding)


def ragged_sizes(rng, number_of, total, most, lean):
    if number_of == 2:
        one = jax.random.randint(rng, (), max(1, total - most), min(most, total - 1) + 1)
        return jnp.stack([one, total - one])
    tallies = jnp.asarray(profile(number_of, total, most, lean), jnp.int32)
    pairs = (number_of - 1) // 2
    donor, receiver = tallies[1:1 + 2 * pairs:2], tallies[2:2 + 2 * pairs:2]
    margin = jnp.minimum(donor - 1, most - receiver)
    moved = jax.random.randint(jax.random.fold_in(rng, 1), (pairs,), 0, 1 << 20) % (margin + 1)
    tallies = tallies.at[1:1 + 2 * pairs:2].set(donor - moved).at[2:2 + 2 * pairs:2].set(receiver + moved)
    return tallies[jax.random.permutation(jax.random.fold_in(rng, 2), number_of)]


def scatter_about(stream_key, dims, width, limit, cuts=(), held_as=jnp.bfloat16):
    factor_of = steps_of(stream_key, dims, cuts, -0.22, 0.18) if cuts else 1.0
    array = jax.random.normal(stream_key, dims, jnp.float32) * width * factor_of
    return jnp.minimum(jnp.maximum(array, -limit), limit).astype(held_as)


def setup_inputs(seed: int = 0) -> dict:
    arg_keys = jax.random.split(jax.random.key(seed), 7)
    return {
        "streams": scatter_about(arg_keys[0], (SEQS, TOKENS, 3, D), 1.0, 6.0, ((0, 4), (1, 64))),
        "cotangent": scatter_about(arg_keys[1], (SEQS, TOKENS, D), 1.0, 6.0, ((0, 4), (1, 64))),
        "doc_ids": jax.vmap(lambda own: jnp.searchsorted(jnp.cumsum(ragged_sizes(own, DOCS, TOKENS, DOC_MOST, 2)), jnp.arange(TOKENS), side="right"))(jax.random.split(arg_keys[2], SEQS)).reshape((SEQS, TOKENS)).astype(jnp.int32),
        "short_taps": scatter_about(arg_keys[3], (3, SHORT, D), SHORT ** -0.5, 3.5, ((2, 64),), jnp.float32),
        "long_taps": scatter_about(arg_keys[4], (GROUPS, LTAPS), LTAPS ** -0.5, 0.5, ((0, 64),), jnp.float32),
        "skip_gain": jnp.clip(0.5 + 1.0 * jax.random.uniform(arg_keys[5], (D,), jnp.float32) ** steps_of(arg_keys[5], (D,), ((0, 64),), -0.2, 0.2), 0.5, 1.5),
    }


def banded(pattern, row_count):
    groups, extent = pattern.shape
    padded = jnp.concatenate([pattern, jnp.zeros((groups, 1), pattern.dtype)], axis=1)
    flattened = jnp.tile(padded, (1, row_count))[:, :row_count * extent]
    return flattened.reshape(groups, row_count, extent)

def windowed(extended, tap_count):
    earlier = extended[:-tap_count].reshape((-1, tap_count) + extended.shape[1:])
    later_rows = extended[tap_count:].reshape((-1, tap_count) + extended.shape[1:])
    return jnp.concatenate([earlier, later_rows], axis=1)

def turn_layout(blocks, groups, turn_limit):
    per_turn = min(4, blocks)
    span_groups = math.gcd(groups, max(1, turn_limit // per_turn))
    return (per_turn, span_groups)

def to_turns(inputs, per_turn, span_groups):
    blocks, row_count, groups, group_width = inputs.shape
    group_spans = groups // span_groups
    reshaped = inputs.reshape(blocks // per_turn, per_turn, row_count, group_spans, span_groups, group_width)
    reshaped = jnp.transpose(reshaped, (3, 0, 1, 2, 4, 5))
    return reshaped.reshape(group_spans * (blocks // per_turn), per_turn, row_count, span_groups, group_width)

def from_turns(result, blocks, groups):
    turn_total, per_turn, row_count, span_groups, group_width = result.shape
    group_spans = groups // span_groups
    merged = result.reshape(group_spans, blocks // per_turn, per_turn, row_count, span_groups, group_width)
    merged = jnp.transpose(merged, (1, 2, 3, 0, 4, 5))
    return merged.reshape(blocks * row_count, groups * group_width)

def ids_to_turns(id_windows, per_turn, group_spans):
    reshaped = id_windows.reshape(-1, per_turn, id_windows.shape[1])
    return jnp.tile(reshaped, (group_spans, 1, 1))

def conv_blocks(extended, id_ext, kernel, own_start, turn_limit):
    groups, tap_count = (kernel.shape[0], kernel.shape[1])
    length = extended.shape[0] - tap_count
    channels = extended.shape[1]
    blocks = length // tap_count
    per_turn, span_groups = turn_layout(blocks, groups, turn_limit)
    block_turns = blocks // per_turn
    group_spans = groups // span_groups
    inputs = windowed(extended, tap_count).reshape(blocks, 2 * tap_count, groups, channels // groups)
    data_turns = to_turns(inputs, per_turn, span_groups)
    id_turns = ids_to_turns(windowed(id_ext, tap_count), per_turn, group_spans)
    kernel_spans = kernel.reshape(group_spans, span_groups, kernel.shape[1], kernel.shape[2])
    span_index = (jnp.arange(group_spans * block_turns, dtype=jnp.int32) // block_turns).astype(jnp.int32)

    def one_turn(operands):
        data_win, ids_win, which = operands
        kernel_part = lax.dynamic_index_in_dim(kernel_spans, which, 0, keepdims=False)
        own_ids = ids_win[:, own_start:own_start + tap_count]
        same_doc = (own_ids[:, :, None] == ids_win[:, None, :]).astype(kernel_part.dtype)
        masked = kernel_part[None] * same_doc[:, None]
        return jnp.einsum('ngts,nsgc->ntgc', masked.astype(jnp.float32), data_win.astype(jnp.float32))
    result = lax.map(one_turn, (data_turns, id_turns, span_index))
    return from_turns(result, blocks, groups)

def long_forward(gated_ext, id_ext, taps16, turn_limit):
    groups, tap_count = taps16.shape
    pattern = jnp.concatenate([jnp.zeros((groups, 1), taps16.dtype), taps16[:, ::-1], jnp.zeros((groups, tap_count - 1), taps16.dtype)], axis=1)
    return conv_blocks(gated_ext, id_ext, banded(pattern, tap_count), tap_count, turn_limit)

def long_backward(grad_ext, id_ext, taps16, turn_limit):
    groups, tap_count = taps16.shape
    pattern = jnp.concatenate([taps16, jnp.zeros((groups, tap_count), taps16.dtype)], axis=1)
    return conv_blocks(grad_ext, id_ext, banded(pattern, tap_count), 0, turn_limit)

def long_taps_grad(grad16, gated_ext, id_ext, groups, turn_limit):
    length, channels = grad16.shape
    tap_count = gated_ext.shape[0] - length
    blocks = length // tap_count
    group_width = channels // groups
    per_turn, span_groups = turn_layout(blocks, groups, turn_limit)
    group_spans = groups // span_groups
    grad_turns = to_turns(grad16.reshape(blocks, tap_count, groups, group_width), per_turn, span_groups)
    data_turns = to_turns(windowed(gated_ext, tap_count).reshape(blocks, 2 * tap_count, groups, group_width), per_turn, span_groups)
    id_turns = ids_to_turns(windowed(id_ext, tap_count), per_turn, group_spans)

    def one_turn(operands):
        grad_part, data_win, ids_win = operands
        product = jnp.einsum('ntgc,nsgc->ngts', grad_part.astype(jnp.float32), data_win.astype(jnp.float32))
        same_doc = (ids_win[:, tap_count:, None] == ids_win[:, None, :]).astype(jnp.float32)
        return lax.optimization_barrier(jnp.sum(product * same_doc[:, None], axis=0))
    partial_sums = lax.map(one_turn, (grad_turns, data_turns, id_turns))
    summed = lax.optimization_barrier(jnp.sum(partial_sums.reshape(group_spans, -1, span_groups, tap_count, 2 * tap_count), axis=1))
    flattened = summed.reshape(groups, tap_count * 2 * tap_count)
    flattened = jnp.concatenate([flattened, jnp.zeros((groups, tap_count), jnp.float32)], axis=1)
    skewed = flattened.reshape(groups, tap_count, 2 * tap_count + 1)
    return lax.optimization_barrier(jnp.sum(skewed[:, :, 1:tap_count + 1], axis=1))[:, ::-1]

def short_forward(stream_ext, id_ext, short_taps):
    short_lead = short_taps.shape[1] - 1
    length = stream_ext.shape[0] - short_lead
    own_ids = id_ext[short_lead:]
    summed = jnp.zeros((length,) + stream_ext.shape[1:], jnp.float32)
    for offset in range(short_lead + 1):
        start_row = short_lead - offset
        same_doc = (id_ext[start_row:start_row + length] == own_ids).astype(jnp.float32)
        summed = summed + short_taps[:, offset][None] * stream_ext[start_row:start_row + length] * same_doc[:, None, None]
    return summed

def short_backward(grad_ext, id_ext, short_taps):
    short_lead = short_taps.shape[1] - 1
    length = grad_ext.shape[0] - short_lead
    own_ids = id_ext[:length]
    summed = jnp.zeros((length,) + grad_ext.shape[1:], jnp.float32)
    for offset in range(short_lead + 1):
        same_doc = (id_ext[offset:offset + length] == own_ids).astype(jnp.float32)
        summed = summed + short_taps[:, offset][None] * grad_ext[offset:offset + length] * same_doc[:, None, None]
    return summed

def short_taps_grad(act_grad, stream_ext, id_ext, short_count):
    short_lead = short_count - 1
    length = act_grad.shape[0]
    own_ids = id_ext[short_lead:]
    pieces = []
    for offset in range(short_count):
        start_row = short_lead - offset
        same_doc = (id_ext[start_row:start_row + length] == own_ids).astype(jnp.float32)
        pieces.append(lax.optimization_barrier(jnp.sum(act_grad * stream_ext[start_row:start_row + length] * same_doc[:, None, None], axis=0)))
    return jnp.stack(pieces, axis=1)

def filler_ids(amount):
    return jnp.full((amount,), -1, jnp.int32)

def one_sequence(streams, cotangent, doc_ids, short_taps, long_taps, skip_gain):
    length, channels = cotangent.shape
    groups, tap_count = long_taps.shape
    short_lead = short_taps.shape[1] - 1
    turn_limit = 1024
    stream_ext = jnp.concatenate([jnp.zeros((short_lead,) + streams.shape[1:], jnp.float32), streams.astype(jnp.float32)], axis=0)
    short_ids = jnp.concatenate([filler_ids(short_lead), doc_ids])
    activated = short_forward(stream_ext, short_ids, short_taps)
    query_act, key_act, value_act = (activated[:, 0], activated[:, 1], activated[:, 2])
    gated_input = key_act * value_act
    gated16 = gated_input.astype(jnp.bfloat16)
    taps16 = long_taps.astype(jnp.bfloat16)
    gated_ext = jnp.concatenate([jnp.zeros((tap_count, channels), jnp.bfloat16), gated16], axis=0)
    long_ids = jnp.concatenate([filler_ids(tap_count), doc_ids])
    convolved = long_forward(gated_ext, long_ids, taps16, turn_limit) + skip_gain * gated_input
    mixed_out = (query_act * convolved).astype(jnp.bfloat16)
    cot_float = cotangent.astype(jnp.float32)
    conv_grad = cot_float * query_act
    conv_grad16 = conv_grad.astype(jnp.bfloat16)
    grad_ext = jnp.concatenate([conv_grad16, jnp.zeros((tap_count, channels), jnp.bfloat16)], axis=0)
    after_ids = jnp.concatenate([doc_ids, filler_ids(tap_count)])
    gated_grad = long_backward(grad_ext, after_ids, taps16, turn_limit) + skip_gain * conv_grad
    taps_grad = long_taps_grad(conv_grad16, gated_ext, long_ids, groups, turn_limit)
    gain_grad = lax.optimization_barrier(jnp.sum(conv_grad * gated_input, axis=0))
    act_grad = jnp.stack([cot_float * convolved, gated_grad * value_act, gated_grad * key_act], axis=1)
    act_ext = jnp.concatenate([act_grad, jnp.zeros((short_lead, 3, channels), jnp.float32)], axis=0)
    stream_grad = short_backward(act_ext, after_ids[:length + short_lead], short_taps).astype(jnp.bfloat16)
    short_grad = short_taps_grad(act_grad, stream_ext, short_ids, short_lead + 1)
    return (mixed_out, stream_grad, short_grad, taps_grad, gain_grad)

def reference(streams, cotangent, doc_ids, short_taps, long_taps, skip_gain):

    def per_sequence(operands):
        return one_sequence(operands[0], operands[1], operands[2], short_taps, long_taps, skip_gain)
    results = lax.map(per_sequence, (streams, cotangent, doc_ids))
    grad_scale = 1.0 / math.sqrt(SEQS * TOKENS)
    short_grad = lax.optimization_barrier(jnp.sum(results[2], axis=0)) * grad_scale
    taps_grad = lax.optimization_barrier(jnp.sum(results[3], axis=0)) * grad_scale
    gain_grad = lax.optimization_barrier(jnp.sum(results[4], axis=0)) * grad_scale
    return (results[0], results[1], short_grad, taps_grad, gain_grad)
```

```python
import functools
import math

import jax
import jax.numpy as jnp
from jax import lax
from jax.experimental import pallas as pl
from jax.experimental.pallas import tpu as pltpu
from jax.sharding import PartitionSpec as P

F32 = jnp.float32
BF16 = jnp.bfloat16
W = 128
PR = 24
CORES = 2


def dot(a, b, dims):
    return lax.dot_general(a, b, (dims, ((), ())), preferred_element_type=F32)


def kernel(
    tiles, chips, dps, scale,
    x_hbm, cot_hbm, ids_ref, short_ref, taps_ref, gain_ref,
    mixed_hbm, grad_hbm, short_out, taps_out, gain_out,
    x, cot, mixed, grad, act, g_own, c_own, g_prev, c_next,
    half, half_in, params, tail, tail_in, idp, idn, edge, edge_in, last,
    part, part_in, block, block_in,
    bmask, fmask, tmask, idx, shift,
    load_sem, half_sem, par_send, par_recv, tail_sem, id_sem,
    g_send, g_recv, c_send, c_recv, e_send, e_recv, r_send, r_recv, b_send, b_recv, out_sem,
):
    per = tiles // chips
    seq = lax.axis_index("seq")
    dp = lax.axis_index("dp")
    chip, core = seq // CORES, lax.rem(seq, CORES)
    n = chips * CORES
    nxt, prv = lax.rem(seq + 1, n), lax.rem(seq + n - 1, n)
    sib = chip * CORES + 1 - core

    def remote(src, dst, send, recv, to, to_dp=None):
        where = {"seq": to} if to_dp is None else {"dp": to_dp, "seq": to}
        return pltpu.make_async_remote_copy(
            src_ref=src, dst_ref=dst, send_sem=send, recv_sem=recv,
            device_id=where, device_id_type=pl.DeviceIdType.MESH,
        )

    def wait_bytes(ref, sem):
        pltpu.make_async_copy(ref, ref, sem).wait()

    load_x = pltpu.make_async_copy(x_hbm, x, load_sem.at[0])
    load_c = pltpu.make_async_copy(cot_hbm, cot, load_sem.at[1])
    load_x.start()
    load_c.start()

    barrier = pltpu.get_barrier_semaphore()

    def greet(to, to_dp=None):
        where = {"seq": to} if to_dp is None else {"dp": to_dp, "seq": to}
        pl.semaphore_signal(barrier, 1, device_id=where, device_id_type=pl.DeviceIdType.MESH)

    greet(nxt)
    greet(prv)
    greet(sib)

    def greet_chip(d, carry):
        greet(lax.rem(chip + d, chips) * CORES + core)
        return carry

    lax.fori_loop(1, chips, greet_chip, 0)

    def greet_dp(d, carry):
        other = lax.rem(dp + d, dps)
        greet(seq, other)
        greet(sib, other)
        return carry

    lax.fori_loop(1, dps, greet_dp, 0)
    pl.semaphore_wait(barrier, 3 + (chips - 1) + 2 * (dps - 1))

    id_to_next = remote(ids_ref, idp, id_sem.at[0], id_sem.at[1], nxt)
    id_to_prev = remote(ids_ref, idn, id_sem.at[2], id_sem.at[3], prv)
    id_to_next.start()
    id_to_prev.start()
    lane = lax.broadcasted_iota(jnp.int32, (16, W), 1)
    row = lax.broadcasted_iota(jnp.int32, (8, W), 0)
    sg = jnp.concatenate(
        [short_ref[...], gain_ref[...], jnp.zeros((6, W // 2), F32)], axis=0
    )
    sg = jnp.where(lane // (W // 2) == core, jnp.concatenate([sg, sg], axis=1), 0.0)
    tp = jnp.where(row // 4 == core, jnp.concatenate([taps_ref[...], taps_ref[...]], axis=0), 0.0)
    for p in range(per):
        half[p, 0:16] = sg
        half[p, 16:24] = tp
    to_sib = remote(half, half_in, half_sem.at[0], half_sem.at[1], sib)
    to_sib.start()

    load_x.wait()
    for i in range(3):
        rows = x[i, W - 16 : W].astype(F32)
        tail[2 * i : 2 * i + 2] = rows[14:16]
    tail[6:8] = jnp.zeros((2, tiles * W), F32)
    tail_to_next = remote(tail, tail_in, tail_sem.at[0], tail_sem.at[1], nxt)
    tail_to_next.start()

    to_sib.wait()
    params[pl.ds(chip * per, per)] = half[...] + half_in[...]

    def send_params(d, carry):
        to = lax.rem(chip + chips + 2 - d, chips)
        to = jnp.where(d == 1, lax.rem(chip + 1, chips), lax.rem(chip + chips + 1 - d, chips))
        mine = params.at[pl.ds(chip * per, per)]
        remote(mine, mine, par_send, par_recv.at[chip], to * CORES + core).start()
        return carry

    lax.fori_loop(1, chips, send_params, 0)

    id_to_next.wait()
    id_to_prev.wait()
    own_row = jnp.broadcast_to(ids_ref[...], (W, W)).astype(F32)
    prev_row = jnp.broadcast_to(jnp.where(seq == 0, -1, idp[...]), (W, W)).astype(F32)
    next_row = jnp.broadcast_to(jnp.where(seq == n - 1, -2, idn[...]), (W, W)).astype(F32)
    own_col, prev_col, next_col = own_row.T, prev_row.T, next_row.T
    s_at = lax.broadcasted_iota(jnp.int32, (W, W), 0)
    t_at = lax.broadcasted_iota(jnp.int32, (W, W), 1)
    same_own = jnp.where((s_at <= t_at) & (own_col == own_row), 1.0, 0.0)
    same_prev = jnp.where((s_at > t_at) & (prev_col == own_row), 1.0, 0.0)
    same_next = jnp.where((s_at > t_at) & (own_col == next_row), 1.0, 0.0)
    bmask[0] = same_own.astype(BF16)
    bmask[1] = same_prev.astype(BF16)
    bmask[2] = same_next.astype(BF16)
    fmask[0] = same_own
    fmask[1] = same_next
    idx[0:8] = prev_col[W - 8 : W]
    idx[8 : W + 8] = own_col
    idx[W + 8 : W + 16] = next_col[0:8]
    mine = idx[8 : W + 8]
    tmask[0] = jnp.where(idx[7 : W + 7] == mine, 1.0, 0.0)
    tmask[1] = jnp.where(idx[6 : W + 6] == mine, 1.0, 0.0)
    tmask[2] = jnp.where(idx[9 : W + 9] == mine, 1.0, 0.0)
    tmask[3] = jnp.where(idx[10 : W + 10] == mine, 1.0, 0.0)
    load_c.wait()
    tail_to_next.wait()

    def forward(i, carry):
        tile = lax.rem((chip + chips - 1) * per + i, tiles)
        owner = tile // per
        lanes = pl.ds(pl.multiple_of(tile * W, W), W)

        @pl.when((lax.rem(tile, per) == 0) & (owner != chip))
        def _():
            wait_bytes(params.at[pl.ds(0, per)], par_recv.at[owner])

        w = params[tile, 0:16]
        m1, m2 = tmask[0], tmask[1]
        for s in range(3):
            now = x[s, :, lanes].astype(F32)
            shift[s, 8 : W + 8] = now
            shift[s, 6:8] = tail_in[2 * s : 2 * s + 2, lanes]
            act[s, :, lanes] = (
                w[3 * s : 3 * s + 1] * now
                + w[3 * s + 1 : 3 * s + 2] * (shift[s, 7 : W + 7] * m1)
                + w[3 * s + 2 : 3 * s + 3] * (shift[s, 6 : W + 6] * m2)
            )
        gated = act[1, :, lanes] * act[2, :, lanes]
        cgrad = cot[:, lanes].astype(F32) * act[0, :, lanes]
        g_own[tile] = gated.astype(BF16).T
        c_own[tile] = cgrad.astype(BF16).T
        remote(g_own.at[tile], g_prev.at[tile], g_send, g_recv.at[tile], nxt).start()
        remote(c_own.at[tile], c_next.at[tile], c_send, c_recv.at[tile], prv).start()
        return carry

    lax.fori_loop(0, tiles, forward, 0)

    shift[:, W + 8 : W + 16] = jnp.zeros((3, 8, W), F32)
    lane_group = lax.broadcasted_iota(jnp.int32, (W, W), 1) // 16
    row8 = lax.broadcasted_iota(jnp.int32, (64, W), 0) % 8

    def backward(i, carry):
        tile = lax.rem(chip * per + i, tiles)
        owner = tile // per
        lanes = pl.ds(pl.multiple_of(tile * W, W), W)
        wait_bytes(g_prev.at[tile], g_recv.at[tile])
        wait_bytes(c_next.at[tile], c_recv.at[tile])
        w = params[tile, 0:16]
        taps = params[tile, 16:24]
        k_own, k_prev, k_next = bmask[0], bmask[1], bmask[2]
        gated = act[1, :, lanes] * act[2, :, lanes]
        g16 = gated.astype(BF16)
        gp, go, co, cn = g_prev[tile], g_own[tile], c_own[tile], c_next[tile]
        cc = jnp.concatenate([co, cn], axis=1)
        gg = jnp.concatenate([gp, go], axis=1)
        conv, back, diag = [], [], []
        for g in range(8):
            spread = jnp.broadcast_to(taps[g : g + 1], (W, W))
            turned = pltpu.roll(spread, 0, 1, stride=1, stride_axis=0).astype(BF16)
            own = turned * k_own
            rows = slice(16 * g, 16 * g + 16)
            conv.append(
                dot(gg[rows], jnp.concatenate([turned * k_prev, own], axis=0), ((1,), (0,)))
            )
            back.append(
                dot(cc[rows], jnp.concatenate([own, turned * k_next], axis=1), ((1,), (1,)))
            )
            pair = dot(jnp.where(lane_group == g, g16, jnp.zeros_like(g16)), cc, ((1,), (0,)))
            pair = pair[:, :W] * fmask[0] + pair[:, W:] * fmask[1]
            total = pair[0:8]
            for q in range(1, W // 8):
                total = total + pltpu.roll(pair[8 * q : 8 * q + 8], W - 8 * q, 1)
            diag.append(total)
        diag = jnp.concatenate(diag, axis=0)
        for bit in (1, 2, 4):
            diag = jnp.where((row8 & bit) != 0, pltpu.roll(diag, W - bit, 1), diag)
        part[tile, 16:24] = jnp.sum(diag.reshape(8, 8, W), axis=1)

        gain = w[9:10]
        q_act, k_act, v_act = act[0, :, lanes], act[1, :, lanes], act[2, :, lanes]
        cotan = cot[:, lanes].astype(F32)
        cgrad = cotan * q_act
        convolved = jnp.concatenate(conv, axis=0).T + gain * gated
        mixed[:, lanes] = (q_act * convolved).astype(BF16)
        ggrad = jnp.concatenate(back, axis=0).T + gain * cgrad
        u1, u2 = tmask[2], tmask[3]
        sums = []
        for s, ag in enumerate((cotan * convolved, ggrad * v_act, ggrad * k_act)):
            shift[s, 8 : W + 8] = ag
            edge[tile, 2 * s : 2 * s + 2] = ag[0:2]
            b1 = shift[s, 9 : W + 9] * u1
            b2 = shift[s, 10 : W + 10] * u2
            sgrad = w[3 * s : 3 * s + 1] * ag + w[3 * s + 1 : 3 * s + 2] * b1 + w[3 * s + 2 : 3 * s + 3] * b2
            grad[s, :, lanes] = sgrad.astype(BF16)
            last[s, :, lanes] = sgrad[W - 16 :]
            now = x[s, :, lanes].astype(F32)
            before = tail_in[2 * s : 2 * s + 2, lanes]
            a1 = ag[0:2] * tmask[0, 0:2]
            a2 = ag[0:2] * tmask[1, 0:2]
            sums.append(jnp.sum(now * ag, axis=0, keepdims=True))
            sums.append(jnp.sum(now * b1, axis=0, keepdims=True) + a1[0:1] * before[1:2])
            sums.append(
                jnp.sum(now * b2, axis=0, keepdims=True) + a2[0:1] * before[0:1] + a2[1:2] * before[1:2]
            )
        sums.append(jnp.sum(cgrad * gated, axis=0, keepdims=True))
        sums.append(jnp.zeros((6, W), F32))
        part[tile, 0:16] = jnp.concatenate(sums, axis=0)
        edge[tile, 6:8] = jnp.zeros((2, W), F32)
        remote(edge.at[tile], edge_in.at[tile], e_send, e_recv, prv).start()

        @pl.when(owner != chip)
        def _():
            slot = part_in.at[lax.rem(tile, per), lax.rem(chip + chips - owner, chips) - 1]
            remote(part.at[tile], slot, r_send, r_recv, owner * CORES + core).start()

        pltpu.make_async_copy(mixed.at[:, lanes], mixed_hbm.at[:, lanes], out_sem.at[0]).start()
        pltpu.make_async_copy(
            grad.at[:, 0 : W - 16, lanes], grad_hbm.at[:, 0 : W - 16, lanes], out_sem.at[1]
        ).start()
        return carry

    lax.fori_loop(0, tiles, backward, 0)

    wait_bytes(part_in, r_recv)
    for p in range(per):
        total = part[chip * per + p]
        for d in range(chips - 1):
            total = total + part_in[p, d]
        block[p] = total

    def send_block(d, carry):
        to_dp = lax.rem(dp + d // CORES, dps)
        to = chip * CORES + lax.rem(core + d, CORES)
        remote(block, block_in.at[d - 1], b_send, b_recv, to, to_dp).start()
        return carry

    lax.fori_loop(1, CORES * dps, send_block, 0)

    wait_bytes(edge_in, e_recv)
    zero14 = jnp.zeros((14, W), F32)

    def finish(tile, carry):
        lanes = pl.ds(pl.multiple_of(tile * W, W), W)
        w = params[tile, 0:16]
        for s in range(3):
            e0 = edge_in[tile, 2 * s : 2 * s + 1]
            e1 = edge_in[tile, 2 * s + 1 : 2 * s + 2]
            w1, w2 = w[3 * s + 1 : 3 * s + 2], w[3 * s + 2 : 3 * s + 3]
            r0 = w2 * (e0 * tmask[3, W - 2 : W - 1])
            r1 = w1 * (e0 * tmask[2, W - 1 : W]) + w2 * (e1 * tmask[3, W - 1 : W])
            more = jnp.concatenate([zero14, r0, r1], axis=0)
            grad[s, W - 16 : W, lanes] = (last[s, :, lanes] + more).astype(BF16)
        return carry

    lax.fori_loop(0, tiles, finish, 0)
    rest = pltpu.make_async_copy(
        grad.at[:, W - 16 : W], grad_hbm.at[:, W - 16 : W], out_sem.at[2]
    )
    rest.start()

    wait_bytes(block_in, b_recv)
    total = block[0]
    for d in range(CORES * dps - 1):
        total = total + block_in[d, 0]
    total = total * scale
    top, low = total[0:16], total[16:24]
    top = jnp.where(core == 0, top, pltpu.roll(top, W // 2, 1))
    short_out[...] = top[0:9, : W // 2]
    gain_out[...] = top[9:10, : W // 2]
    taps_out[...] = jnp.where(core == 0, low[0:4], low[4:8])

    wait_bytes(params.at[pl.ds(0, (chips - 1) * per)], par_send)
    wait_bytes(g_own, g_send)
    wait_bytes(c_own, c_send)
    wait_bytes(edge, e_send)
    wait_bytes(part.at[pl.ds(0, (chips - 1) * per)], r_send)
    wait_bytes(block_in, b_send)
    wait_bytes(mixed, out_sem.at[0])
    wait_bytes(grad.at[:, 0 : W - 16], out_sem.at[1])
    rest.wait()


def local(streams, cotangent, doc_ids, short_taps, long_taps, skip_gain):
    channels = cotangent.shape[2]
    n, dps = lax.axis_size("seq"), lax.axis_size("dp")
    tiles, chips = channels // W, n // CORES
    per = tiles // chips
    x = jnp.transpose(streams[0], (1, 0, 2))
    scale = 1.0 / math.sqrt(dps * n * W)
    dma, vmem = pltpu.SemaphoreType.DMA, pltpu.VMEM
    any_, inv = pl.BlockSpec(memory_space=pl.ANY), pl.BlockSpec(memory_space=pltpu.VMEM)
    mixed, grad, short_grad, taps_grad, gain_grad = pl.pallas_call(
        functools.partial(kernel, tiles, chips, dps, scale),
        out_shape=(
            jax.ShapeDtypeStruct((W, channels), BF16),
            jax.ShapeDtypeStruct((3, W, channels), BF16),
            jax.ShapeDtypeStruct((9, W // 2), F32),
            jax.ShapeDtypeStruct((4, W), F32),
            jax.ShapeDtypeStruct((1, W // 2), F32),
        ),
        in_specs=[any_, any_, inv, inv, inv, inv],
        out_specs=(any_, any_, inv, inv, inv),
        scratch_shapes=[
            vmem((3, W, channels), BF16),
            vmem((W, channels), BF16),
            vmem((W, channels), BF16),
            vmem((3, W, channels), BF16),
            vmem((3, W, channels), F32),
            vmem((tiles, W, W), BF16),
            vmem((tiles, W, W), BF16),
            vmem((tiles, W, W), BF16),
            vmem((tiles, W, W), BF16),
            vmem((per, PR, W), F32),
            vmem((per, PR, W), F32),
            vmem((tiles, PR, W), F32),
            vmem((8, channels), F32),
            vmem((8, channels), F32),
            vmem((1, W), jnp.int32),
            vmem((1, W), jnp.int32),
            vmem((tiles, 8, W), F32),
            vmem((tiles, 8, W), F32),
            vmem((3, 16, channels), F32),
            vmem((tiles, PR, W), F32),
            vmem((per, chips - 1, PR, W), F32),
            vmem((per, PR, W), F32),
            vmem((CORES * dps - 1, per, PR, W), F32),
            vmem((3, W, W), BF16),
            vmem((2, W, W), F32),
            vmem((4, W, W), F32),
            vmem((W + 16, W), F32),
            vmem((3, W + 16, W), F32),
            dma((2,)),
            dma((2,)),
            dma(()),
            dma((chips,)),
            dma((2,)),
            dma((4,)),
            dma(()),
            dma((tiles,)),
            dma(()),
            dma((tiles,)),
            dma(()),
            dma(()),
            dma(()),
            dma(()),
            dma(()),
            dma(()),
            dma((3,)),
        ],
        compiler_params=pltpu.CompilerParams(
            collective_id=0, has_side_effects=True, vmem_limit_bytes=48 * 1024 * 1024
        ),
        cost_estimate=pl.CostEstimate(
            flops=6 * W * W * channels, bytes_accessed=16 * W * channels, transcendentals=0
        ),
        name="hyena_block",
    )(
        x,
        cotangent[0],
        doc_ids,
        short_taps.reshape(9, -1)[:, : W // 2],
        long_taps[:4],
        skip_gain.reshape(1, -1)[:, : W // 2],
    )
    return (
        mixed[None],
        jnp.transpose(grad, (1, 0, 2))[None],
        short_grad.reshape(3, 3, W // 2),
        taps_grad,
        gain_grad.reshape(W // 2),
    )


def solution(mesh):
    return jax.shard_map(
        local,
        mesh=mesh,
        in_specs=(
            P("dp", "seq", None, None),
            P("dp", "seq", None),
            P("dp", "seq"),
            P(None, None, "seq"),
            P("seq", None),
            P("seq"),
        ),
        out_specs=(
            P("dp", "seq", None),
            P("dp", "seq", None, None),
            P(None, None, "seq"),
            P("seq", None),
            P("seq"),
        ),
        check_vma=False,
    )
```

```python
import functools
import math

import jax
import jax.numpy as jnp
from jax import lax
from jax.experimental import pallas as pl
from jax.experimental.pallas import tpu as pltpu
from jax.sharding import PartitionSpec as P

F32 = jnp.float32
BF16 = jnp.bfloat16
W = 128
PR = 18
CORES = 2


def dot(a, b, dims):
    return lax.dot_general(a, b, (dims, ((), ())), preferred_element_type=F32)


def kernel(
    tiles, chips, dps, scale,
    x_hbm, cot_hbm, ids_hbm, short_hbm, taps_hbm, gain_hbm,
    out, small_out,
    x, cot, ids_ref, short_ref, taps_ref, gain_ref, act, g_own, c_own, g_prev, c_next,
    half, half_in, params, tail, tail_in, idp, idn, edge, edge_in, last,
    part, part_in, block, block_in,
    bmask, perm, turn, rtaps, tmask, idx, shift,
    load_sem, half_sem, par_send, par_pass, par_recv, tail_sem, id_sem,
    g_send, g_recv, c_send, c_recv, e_send, e_recv, r_send, r_recv, b_send, b_recv,
):
    per = tiles // chips
    seq = lax.axis_index("seq")
    dp = lax.axis_index("dp")
    chip, core = seq // CORES, lax.rem(seq, CORES)
    n = chips * CORES
    nxt, prv = lax.rem(seq + 1, n), lax.rem(seq + n - 1, n)
    sib = chip * CORES + 1 - core

    def remote(src, dst, send, recv, to, to_dp=None):
        where = {"seq": to} if to_dp is None else {"dp": to_dp, "seq": to}
        return pltpu.make_async_remote_copy(
            src_ref=src, dst_ref=dst, send_sem=send, recv_sem=recv,
            device_id=where, device_id_type=pl.DeviceIdType.MESH,
        )

    def wait_bytes(ref, sem):
        pltpu.make_async_copy(ref, ref, sem).wait()

    load_x = pltpu.make_async_copy(x_hbm, x, load_sem.at[0])
    load_c = pltpu.make_async_copy(cot_hbm, cot, load_sem.at[1])
    small = [
        pltpu.make_async_copy(a, b, load_sem.at[2 + q])
        for q, (a, b) in enumerate(
            ((ids_hbm, ids_ref), (short_hbm, short_ref), (taps_hbm, taps_ref), (gain_hbm, gain_ref))
        )
    ]
    for copy in small:
        copy.start()
    load_x.start()
    load_c.start()
    peers = dps * CORES
    place = dp * CORES + core

    barrier = pltpu.get_barrier_semaphore()

    def greet(to, to_dp=None):
        where = {"seq": to} if to_dp is None else {"dp": to_dp, "seq": to}
        pl.semaphore_signal(barrier, 1, device_id=where, device_id_type=pl.DeviceIdType.MESH)

    greet(nxt)
    greet(prv)
    greet(sib)

    def greet_chip(d, carry):
        greet(lax.rem(chip + d, chips) * CORES + core)
        return carry

    lax.fori_loop(1, chips, greet_chip, 0)

    def greet_dp(d, carry):
        other = lax.rem(dp + d, dps)
        greet(seq, other)
        greet(sib, other)
        return carry

    lax.fori_loop(1, dps, greet_dp, 0)
    pl.semaphore_wait(barrier, 3 + (chips - 1) + 2 * (dps - 1))

    for copy in small:
        copy.wait()
    id_to_next = remote(ids_ref, idp, id_sem.at[0], id_sem.at[1], nxt)
    id_to_prev = remote(ids_ref, idn, id_sem.at[2], id_sem.at[3], prv)
    id_to_next.start()
    id_to_prev.start()
    lane = lax.broadcasted_iota(jnp.int32, (10, W), 1)
    row = lax.broadcasted_iota(jnp.int32, (8, W), 0)
    sg = jnp.concatenate([short_ref[0], short_ref[1], short_ref[2], gain_ref[...]], axis=0)[:, : W // 2]
    sg = jnp.where(lane // (W // 2) == core, jnp.concatenate([sg, sg], axis=1), 0.0)
    tp = taps_ref[0:4]
    tp = jnp.where(row // 4 == core, jnp.concatenate([tp, tp], axis=0), 0.0)
    for p in range(per):
        half[p, 0:10] = sg
        half[p, 10:18] = tp
    to_sib = remote(half, half_in, half_sem.at[0], half_sem.at[1], sib)
    to_sib.start()

    load_x.wait()
    for i in range(3):
        rows = x[i, W - 16 : W].astype(F32)
        tail[2 * i : 2 * i + 2] = rows[14:16]
    tail[6:8] = jnp.zeros((2, tiles * W), F32)
    tail_to_next = remote(tail, tail_in, tail_sem.at[0], tail_sem.at[1], nxt)
    tail_to_next.start()

    to_sib.wait()
    params[pl.ds(chip * per, per)] = half[...] + half_in[...]

    rounds = -(-chips // peers)

    def each_round(act_on):
        def body(m, carry):
            d = place + peers * m

            @pl.when((d > 0) & (d < chips))
            def _():
                act_on(d)

            return carry

        lax.fori_loop(0, rounds, body, 0)

    def send_params(d):
        mine = params.at[pl.ds(chip * per, per)]
        to = lax.rem(chip + d, chips) * CORES + core
        remote(mine, mine, par_send.at[d], par_recv.at[chip], to).start()

    def pass_params(d):
        source = lax.rem(chip + chips - d, chips)
        mine = params.at[pl.ds(source * per, per)]
        wait_bytes(mine, par_recv.at[source])

        def one(e, carry):
            peer = lax.rem(place + e, peers)
            to = chip * CORES + lax.rem(peer, CORES)
            remote(mine, mine, par_pass.at[d], par_recv.at[source], to, peer // CORES).start()
            return carry

        lax.fori_loop(1, peers, one, 0)

    each_round(send_params)

    id_to_next.wait()
    id_to_prev.wait()
    own_row = jnp.broadcast_to(ids_ref[...], (W, W)).astype(F32)
    prev_row = jnp.broadcast_to(jnp.where(seq == 0, -1, idp[...]), (W, W)).astype(F32)
    next_row = jnp.broadcast_to(jnp.where(seq == n - 1, -2, idn[...]), (W, W)).astype(F32)
    own_col, prev_col, next_col = own_row.T, prev_row.T, next_row.T
    s_at = lax.broadcasted_iota(jnp.int32, (W, W), 0)
    t_at = lax.broadcasted_iota(jnp.int32, (W, W), 1)
    same_own = jnp.where((s_at <= t_at) & (own_col == own_row), 1.0, 0.0)
    same_prev = jnp.where((s_at > t_at) & (prev_col == own_row), 1.0, 0.0)
    same_next = jnp.where((s_at > t_at) & (own_col == next_row), 1.0, 0.0)
    bmask[0] = same_own.astype(BF16)
    bmask[1] = same_prev.astype(BF16)
    bmask[2] = same_next.astype(BF16)
    bmask[3] = same_own.T.astype(BF16)
    bmask[4] = same_next.T.astype(BF16)
    turn[...] = jnp.where((s_at + t_at) % W == 0, 1.0, 0.0).astype(BF16)
    for q in range(8):
        perm[q * W : q * W + W] = jnp.where(
            (s_at + t_at + 1 - 16 * q) % W == 0, 1.0, 0.0
        ).astype(BF16)
    idx[0:8] = prev_col[W - 8 : W]
    idx[8 : W + 8] = own_col
    idx[W + 8 : W + 16] = next_col[0:8]
    mine = idx[8 : W + 8]
    tmask[0] = jnp.where(idx[7 : W + 7] == mine, 1.0, 0.0)
    tmask[1] = jnp.where(idx[6 : W + 6] == mine, 1.0, 0.0)
    tmask[2] = jnp.where(idx[9 : W + 9] == mine, 1.0, 0.0)
    tmask[3] = jnp.where(idx[10 : W + 10] == mine, 1.0, 0.0)
    each_round(pass_params)
    load_c.wait()
    tail_to_next.wait()

    def forward(i, carry):
        tile = lax.rem((chip + chips - 1) * per + i, tiles)
        owner = tile // per
        lanes = pl.ds(pl.multiple_of(tile * W, W), W)

        far = lax.rem(chip + chips - owner, chips)

        @pl.when((lax.rem(tile, per) == 0) & (lax.rem(far, peers) != place) & (far != 0))
        def _():
            wait_bytes(params.at[pl.ds(0, per)], par_recv.at[owner])

        w = params[tile, 0:10]
        rtaps[tile] = dot(params[tile, 10:18].astype(BF16), turn[...], ((1,), (0,)))
        m1, m2 = tmask[0], tmask[1]
        for s in range(3):
            now = x[s, :, lanes].astype(F32)
            shift[s, 8 : W + 8] = now
            shift[s, 6:8] = tail_in[2 * s : 2 * s + 2, lanes]
            act[s, :, lanes] = (
                w[3 * s : 3 * s + 1] * now
                + w[3 * s + 1 : 3 * s + 2] * (shift[s, 7 : W + 7] * m1)
                + w[3 * s + 2 : 3 * s + 3] * (shift[s, 6 : W + 6] * m2)
            )
        gated = act[1, :, lanes] * act[2, :, lanes]
        cgrad = cot[:, lanes].astype(F32) * act[0, :, lanes]
        g_own[tile] = gated.astype(BF16).T
        c_own[tile] = cgrad.astype(BF16).T
        remote(g_own.at[tile], g_prev.at[tile], g_send, g_recv.at[tile], nxt).start()
        remote(c_own.at[tile], c_next.at[tile], c_send, c_recv.at[tile], prv).start()
        return carry

    lax.fori_loop(0, tiles, forward, 0)

    shift[:, W + 8 : W + 16] = jnp.zeros((3, 8, W), F32)
    lane_group = lax.broadcasted_iota(jnp.int32, (W, W), 1) // 16

    def circulant(row):
        spread = jnp.broadcast_to(row, (W, W))
        return pltpu.roll(spread, 0, 1, stride=1, stride_axis=0).astype(BF16)

    def backward(i, carry):
        tile = lax.rem(chip * per + i, tiles)
        owner = tile // per
        lanes = pl.ds(pl.multiple_of(tile * W, W), W)
        wait_bytes(g_prev.at[tile], g_recv.at[tile])
        wait_bytes(c_next.at[tile], c_recv.at[tile])
        w = params[tile, 0:10]
        taps = params[tile, 10:18]
        flipped = rtaps[tile]
        k_own, k_prev, k_next, o_own, o_next = [bmask[q] for q in range(5)]
        gated = act[1, :, lanes] * act[2, :, lanes]
        g16 = gated.astype(BF16)
        cc = jnp.concatenate([c_own[tile], c_next[tile]], axis=1)
        gg = jnp.concatenate([g_prev[tile], g_own[tile]], axis=1)
        conv, back, pairs = [], [], []
        for g in range(8):
            fwd = circulant(taps[g : g + 1])
            rev = circulant(flipped[g : g + 1])
            rows = slice(16 * g, 16 * g + 16)
            conv.append(
                dot(gg[rows], jnp.concatenate([fwd * k_prev, fwd * k_own], axis=0), ((1,), (0,)))
            )
            back.append(
                dot(cc[rows], jnp.concatenate([rev * o_own, rev * o_next], axis=0), ((1,), (0,)))
            )
            pair = dot(jnp.where(lane_group == g, g16, jnp.zeros_like(g16)), cc, ((1,), (0,)))
            pair = pair.astype(BF16)
            pairs.append(pair[:, :W] * k_own + pair[:, W:] * k_next)
        lined = jnp.concatenate(
            [
                jnp.concatenate([pair[16 * q : 16 * q + 16] for pair in pairs], axis=0)
                for q in range(8)
            ],
            axis=1,
        )
        diag = dot(lined, perm[...], ((1,), (0,)))
        diag = [
            jnp.sum(
                pltpu.roll(diag[16 * g : 16 * g + 16], 0, 1, stride=1, stride_axis=0),
                axis=0, keepdims=True,
            )
            for g in range(8)
        ]
        part[tile, 10:18] = jnp.concatenate(diag, axis=0)

        gain = w[9:10]
        q_act, k_act, v_act = act[0, :, lanes], act[1, :, lanes], act[2, :, lanes]
        cotan = cot[:, lanes].astype(F32)
        cgrad = cotan * q_act
        convolved = jnp.concatenate(conv, axis=0).T + gain * gated
        out[0, :, lanes] = (q_act * convolved).astype(BF16)
        ggrad = jnp.concatenate(back, axis=0).T + gain * cgrad
        u1, u2 = tmask[2], tmask[3]
        sums = []
        for s, ag in enumerate((cotan * convolved, ggrad * v_act, ggrad * k_act)):
            shift[s, 8 : W + 8] = ag
            edge[tile, 2 * s : 2 * s + 2] = ag[0:2]
            b1 = shift[s, 9 : W + 9] * u1
            b2 = shift[s, 10 : W + 10] * u2
            sgrad = w[3 * s : 3 * s + 1] * ag + w[3 * s + 1 : 3 * s + 2] * b1 + w[3 * s + 2 : 3 * s + 3] * b2
            out[s + 1, :, lanes] = sgrad.astype(BF16)
            last[s, :, lanes] = sgrad[W - 16 :]
            now = x[s, :, lanes].astype(F32)
            before = tail_in[2 * s : 2 * s + 2, lanes]
            a1 = ag[0:2] * tmask[0, 0:2]
            a2 = ag[0:2] * tmask[1, 0:2]
            sums.append(jnp.sum(now * ag, axis=0, keepdims=True))
            sums.append(jnp.sum(now * b1, axis=0, keepdims=True) + a1[0:1] * before[1:2])
            sums.append(
                jnp.sum(now * b2, axis=0, keepdims=True) + a2[0:1] * before[0:1] + a2[1:2] * before[1:2]
            )
        sums.append(jnp.sum(cgrad * gated, axis=0, keepdims=True))
        part[tile, 0:10] = jnp.concatenate(sums, axis=0)
        edge[tile, 6:8] = jnp.zeros((2, W), F32)
        remote(edge.at[tile], edge_in.at[tile], e_send, e_recv, prv).start()

        @pl.when(owner != chip)
        def _():
            slot = part_in.at[lax.rem(tile, per), lax.rem(chip + chips - owner, chips) - 1]
            remote(part.at[tile], slot, r_send, r_recv, owner * CORES + core).start()

        return carry

    lax.fori_loop(0, tiles, backward, 0)

    wait_bytes(part_in, r_recv)
    for p in range(per):
        total = part[chip * per + p]
        for d in range(chips - 1):
            total = total + part_in[p, d]
        block[p] = total

    def send_block(d, carry):
        to_dp = lax.rem(dp + d // CORES, dps)
        to = chip * CORES + lax.rem(core + d, CORES)
        remote(block, block_in.at[d - 1], b_send, b_recv, to, to_dp).start()
        return carry

    lax.fori_loop(1, CORES * dps, send_block, 0)

    wait_bytes(edge_in, e_recv)
    zero14 = jnp.zeros((14, W), F32)

    def finish(tile, carry):
        lanes = pl.ds(pl.multiple_of(tile * W, W), W)
        w = params[tile, 0:10]
        for s in range(3):
            e0 = edge_in[tile, 2 * s : 2 * s + 1]
            e1 = edge_in[tile, 2 * s + 1 : 2 * s + 2]
            w1, w2 = w[3 * s + 1 : 3 * s + 2], w[3 * s + 2 : 3 * s + 3]
            r0 = w2 * (e0 * tmask[3, W - 2 : W - 1])
            r1 = w1 * (e0 * tmask[2, W - 1 : W]) + w2 * (e1 * tmask[3, W - 1 : W])
            more = jnp.concatenate([zero14, r0, r1], axis=0)
            out[s + 1, W - 16 : W, lanes] = (last[s, :, lanes] + more).astype(BF16)
        return carry

    lax.fori_loop(0, tiles, finish, 0)
    wait_bytes(block_in, b_recv)
    total = block[0]
    for d in range(CORES * dps - 1):
        total = total + block_in[d, 0]
    total = total * scale
    top, low = total[0:10], total[10:18]
    small_out[0:10] = jnp.where(core == 0, top, pltpu.roll(top, W // 2, 1))
    small_out[16:20] = jnp.where(core == 0, low[0:4], low[4:8])
    small_out[20:24] = jnp.zeros((4, W), F32)

    def sent_params(d):
        wait_bytes(params.at[pl.ds(0, per)], par_send.at[d])
        wait_bytes(block_in, par_pass.at[d])

    each_round(sent_params)
    wait_bytes(g_own, g_send)
    wait_bytes(c_own, c_send)
    wait_bytes(edge, e_send)
    wait_bytes(part.at[pl.ds(0, (chips - 1) * per)], r_send)
    wait_bytes(block_in, b_send)


def hand_over(out, small, mixed, grad, short_grad, taps_grad, gain_grad, sem):
    copies = [pltpu.make_async_copy(out.at[0], mixed, sem.at[0])]
    for s in range(3):
        copies.append(pltpu.make_async_copy(out.at[s + 1], grad.at[s], sem.at[s + 1]))
    for copy in copies:
        copy.start()
    for s in range(3):
        short_grad[s] = small[3 * s : 3 * s + 3, : W // 2]
    gain_grad[...] = small[9:10, : W // 2]
    s_at = lax.broadcasted_iota(jnp.int32, (W, W), 0)
    t_at = lax.broadcasted_iota(jnp.int32, (W, W), 1)
    flip = jnp.where(s_at + t_at == W - 1, 1.0, 0.0)
    taps_grad[...] = lax.dot_general(
        small[16:24], flip, (((1,), (0,)), ((), ())),
        precision=lax.Precision.HIGHEST, preferred_element_type=F32,
    )[0:4]
    for copy in copies:
        copy.wait()


def local(streams, cotangent, doc_ids, short_taps, long_taps, skip_gain):
    channels = cotangent.shape[2]
    n, dps = lax.axis_size("seq"), lax.axis_size("dp")
    tiles, chips = channels // W, n // CORES
    per = tiles // chips
    x = jnp.transpose(streams[0], (1, 0, 2))
    scale = 1.0 / math.sqrt(dps * n * W)
    dma, vmem = pltpu.SemaphoreType.DMA, pltpu.VMEM
    any_, inv = pl.BlockSpec(memory_space=pltpu.HBM), pl.BlockSpec(memory_space=pltpu.VMEM)
    out, small = pl.pallas_call(
        functools.partial(kernel, tiles, chips, dps, scale),
        out_shape=(
            jax.ShapeDtypeStruct((4, W, channels), BF16),
            jax.ShapeDtypeStruct((24, W), F32),
        ),
        in_specs=[any_] * 6,
        out_specs=(inv, inv),
        scratch_shapes=[
            vmem((3, W, channels), BF16),
            vmem((W, channels), BF16),
            vmem(doc_ids.shape, jnp.int32),
            vmem(short_taps.shape, F32),
            vmem(long_taps.shape, F32),
            vmem((1,) + skip_gain.shape, F32),
            vmem((3, W, channels), F32),
            vmem((tiles, W, W), BF16),
            vmem((tiles, W, W), BF16),
            vmem((tiles, W, W), BF16),
            vmem((tiles, W, W), BF16),
            vmem((per, PR, W), F32),
            vmem((per, PR, W), F32),
            vmem((tiles, PR, W), F32),
            vmem((8, channels), F32),
            vmem((8, channels), F32),
            vmem((1, W), jnp.int32),
            vmem((1, W), jnp.int32),
            vmem((tiles, 8, W), F32),
            vmem((tiles, 8, W), F32),
            vmem((3, 16, channels), F32),
            vmem((tiles, PR, W), F32),
            vmem((per, chips - 1, PR, W), F32),
            vmem((per, PR, W), F32),
            vmem((CORES * dps - 1, per, PR, W), F32),
            vmem((5, W, W), BF16),
            vmem((8 * W, W), BF16),
            vmem((W, W), BF16),
            vmem((tiles, 8, W), F32),
            vmem((4, W, W), F32),
            vmem((W + 16, W), F32),
            vmem((3, W + 16, W), F32),
            dma((6,)),
            dma((2,)),
            dma((chips,)),
            dma((chips,)),
            dma((chips,)),
            dma((2,)),
            dma((4,)),
            dma(()),
            dma((tiles,)),
            dma(()),
            dma((tiles,)),
            dma(()),
            dma(()),
            dma(()),
            dma(()),
            dma(()),
            dma(()),
        ],
        compiler_params=pltpu.CompilerParams(
            collective_id=0, has_side_effects=True, vmem_limit_bytes=32 * 1024 * 1024
        ),
        cost_estimate=pl.CostEstimate(
            flops=6 * W * W * channels, bytes_accessed=16 * W * channels, transcendentals=0
        ),
        name="hyena_block",
    )(
        *(
            pltpu.with_memory_space_constraint(a, pltpu.HBM)
            for a in (x, cotangent[0], doc_ids, short_taps, long_taps, skip_gain.reshape(1, -1))
        )
    )
    mixed, grad, short_grad, taps_grad, gain_grad = pl.pallas_call(
        hand_over,
        out_shape=(
            jax.ShapeDtypeStruct((W, channels), BF16),
            jax.ShapeDtypeStruct((3, W, channels), BF16),
            jax.ShapeDtypeStruct((3, 3, W // 2), F32),
            jax.ShapeDtypeStruct((4, W), F32),
            jax.ShapeDtypeStruct((1, W // 2), F32),
        ),
        in_specs=[inv, inv],
        out_specs=(any_, any_, inv, inv, inv),
        scratch_shapes=[dma((4,))],
        compiler_params=pltpu.CompilerParams(vmem_limit_bytes=16 * 1024 * 1024),
        name="hand_over",
    )(out, small)
    return (
        mixed[None],
        jnp.transpose(grad, (1, 0, 2))[None],
        short_grad,
        taps_grad,
        gain_grad.reshape(W // 2),
    )


def solution(mesh):
    return jax.shard_map(
        local,
        mesh=mesh,
        in_specs=(
            P("dp", "seq", None, None),
            P("dp", "seq", None),
            P("dp", "seq"),
            P(None, None, "seq"),
            P("seq", None),
            P("seq"),
        ),
        out_specs=(
            P("dp", "seq", None),
            P("dp", "seq", None, None),
            P(None, None, "seq"),
            P("seq", None),
            P("seq"),
        ),
        check_vma=False,
    )
```

```python
import functools
import math

import jax
import jax.numpy as jnp
from jax import lax
from jax.experimental import pallas as pl
from jax.experimental.pallas import tpu as pltpu
from jax.sharding import PartitionSpec as P

F32 = jnp.float32
BF16 = jnp.bfloat16
W = 128
PR = 18
CORES = 2
STEP = 32


def dot(a, b, dims):
    return lax.dot_general(a, b, (dims, ((), ())), preferred_element_type=F32)


def kernel(
    tiles, chips, dps, scale,
    x_hbm, cot_hbm, ids_hbm, short_hbm, taps_hbm, gain_hbm,
    out, small_out,
    x, cot, ids_ref, short_ref, taps_ref, gain_ref, act, g_own, c_own, g_prev, c_next,
    half, half_in, params, tail, tail_in, idp, idn, edge, edge_in, last,
    part, part_in, block, block_in,
    bmask, perm, turn, rtaps, tmask, idx, shift, sums_t, turned, flat,
    load_sem, half_sem, par_send, par_pass, par_recv, tail_sem, id_sem,
    g_send, g_recv, c_send, c_recv, e_send, e_recv, r_send, r_recv, b_send, b_recv,
):
    per = tiles // chips
    seq = lax.axis_index("seq")
    dp = lax.axis_index("dp")
    chip, core = seq // CORES, lax.rem(seq, CORES)
    n = chips * CORES
    nxt, prv = lax.rem(seq + 1, n), lax.rem(seq + n - 1, n)
    sib = chip * CORES + 1 - core

    def remote(src, dst, send, recv, to, to_dp=None):
        where = {"seq": to} if to_dp is None else {"dp": to_dp, "seq": to}
        return pltpu.make_async_remote_copy(
            src_ref=src, dst_ref=dst, send_sem=send, recv_sem=recv,
            device_id=where, device_id_type=pl.DeviceIdType.MESH,
        )

    def wait_bytes(ref, sem):
        pltpu.make_async_copy(ref, ref, sem).wait()

    load_x = pltpu.make_async_copy(x_hbm, x, load_sem.at[0])
    load_c = pltpu.make_async_copy(cot_hbm, cot, load_sem.at[1])
    small = [
        pltpu.make_async_copy(a, b, load_sem.at[2 + q])
        for q, (a, b) in enumerate(
            ((ids_hbm, ids_ref), (short_hbm, short_ref), (taps_hbm, taps_ref), (gain_hbm, gain_ref))
        )
    ]
    for copy in small:
        copy.start()
    load_x.start()
    load_c.start()
    peers = dps * CORES
    place = dp * CORES + core

    barrier = pltpu.get_barrier_semaphore()

    def greet(to, to_dp=None):
        where = {"seq": to} if to_dp is None else {"dp": to_dp, "seq": to}
        pl.semaphore_signal(barrier, 1, device_id=where, device_id_type=pl.DeviceIdType.MESH)

    greet(nxt)
    greet(prv)
    greet(sib)

    def greet_chip(d, carry):
        greet(lax.rem(chip + d, chips) * CORES + core)
        return carry

    lax.fori_loop(1, chips, greet_chip, 0)

    def greet_dp(d, carry):
        other = lax.rem(dp + d, dps)
        greet(seq, other)
        greet(sib, other)
        return carry

    lax.fori_loop(1, dps, greet_dp, 0)
    pl.semaphore_wait(barrier, 3 + (chips - 1) + 2 * (dps - 1))

    for copy in small:
        copy.wait()
    id_to_next = remote(ids_ref, idp, id_sem.at[0], id_sem.at[1], nxt)
    id_to_prev = remote(ids_ref, idn, id_sem.at[2], id_sem.at[3], prv)
    id_to_next.start()
    id_to_prev.start()
    lane = lax.broadcasted_iota(jnp.int32, (10, W), 1)
    row = lax.broadcasted_iota(jnp.int32, (8, W), 0)
    sg = jnp.concatenate([short_ref[0], short_ref[1], short_ref[2], gain_ref[...]], axis=0)[:, : W // 2]
    sg = jnp.where(lane // (W // 2) == core, jnp.concatenate([sg, sg], axis=1), 0.0)
    tp = taps_ref[0:4]
    tp = jnp.where(row // 4 == core, jnp.concatenate([tp, tp], axis=0), 0.0)
    for p in range(per):
        half[p, 0:10] = sg
        half[p, 10:18] = tp
    to_sib = remote(half, half_in, half_sem.at[0], half_sem.at[1], sib)
    to_sib.start()

    load_x.wait()
    for i in range(3):
        rows = x[i, W - 16 : W].astype(F32)
        tail[2 * i : 2 * i + 2] = rows[14:16]
    tail[6:8] = jnp.zeros((2, tiles * W), F32)
    tail_to_next = remote(tail, tail_in, tail_sem.at[0], tail_sem.at[1], nxt)
    tail_to_next.start()

    to_sib.wait()
    params[pl.ds(chip * per, per)] = half[...] + half_in[...]

    rounds = -(-chips // peers)

    def each_round(act_on):
        def body(m, carry):
            d = place + peers * m

            @pl.when((d > 0) & (d < chips))
            def _():
                act_on(d)

            return carry

        lax.fori_loop(0, rounds, body, 0)

    def send_params(d):
        mine = params.at[pl.ds(chip * per, per)]
        to = lax.rem(chip + d, chips) * CORES + core
        remote(mine, mine, par_send.at[d], par_recv.at[chip], to).start()

    def pass_params(d):
        source = lax.rem(chip + chips - d, chips)
        mine = params.at[pl.ds(source * per, per)]
        wait_bytes(mine, par_recv.at[source])

        def one(e, carry):
            peer = lax.rem(place + e, peers)
            to = chip * CORES + lax.rem(peer, CORES)
            remote(mine, mine, par_pass.at[d], par_recv.at[source], to, peer // CORES).start()
            return carry

        lax.fori_loop(1, peers, one, 0)

    each_round(send_params)

    id_to_next.wait()
    id_to_prev.wait()
    own_row = jnp.broadcast_to(ids_ref[...], (W, W)).astype(F32)
    prev_row = jnp.broadcast_to(jnp.where(seq == 0, -1, idp[...]), (W, W)).astype(F32)
    next_row = jnp.broadcast_to(jnp.where(seq == n - 1, -2, idn[...]), (W, W)).astype(F32)
    own_col, prev_col, next_col = own_row.T, prev_row.T, next_row.T
    s_at = lax.broadcasted_iota(jnp.int32, (W, W), 0)
    t_at = lax.broadcasted_iota(jnp.int32, (W, W), 1)
    same_own = jnp.where((s_at <= t_at) & (own_col == own_row), 1.0, 0.0)
    same_prev = jnp.where((s_at > t_at) & (prev_col == own_row), 1.0, 0.0)
    same_next = jnp.where((s_at > t_at) & (own_col == next_row), 1.0, 0.0)
    bmask[0] = same_own.astype(BF16)
    bmask[1] = same_prev.astype(BF16)
    bmask[2] = same_next.astype(BF16)
    bmask[3] = same_own.T.astype(BF16)
    bmask[4] = same_next.T.astype(BF16)
    turn[...] = jnp.where((s_at + t_at) % W == 0, 1.0, 0.0).astype(BF16)
    for q in range(8):
        perm[q * W : q * W + W] = jnp.where(
            (s_at + t_at + 1 - 16 * q) % W == 0, 1.0, 0.0
        ).astype(BF16)
    idx[0:8] = prev_col[W - 8 : W]
    idx[8 : W + 8] = own_col
    idx[W + 8 : W + 16] = next_col[0:8]
    mine = idx[8 : W + 8]
    tmask[0] = jnp.where(idx[7 : W + 7] == mine, 1.0, 0.0)
    tmask[1] = jnp.where(idx[6 : W + 6] == mine, 1.0, 0.0)
    tmask[2] = jnp.where(idx[9 : W + 9] == mine, 1.0, 0.0)
    tmask[3] = jnp.where(idx[10 : W + 10] == mine, 1.0, 0.0)
    each_round(pass_params)
    load_c.wait()
    tail_to_next.wait()

    def get_params(i):
        tile = lax.rem((chip + chips - 1) * per + i, tiles)
        owner = tile // per

        far = lax.rem(chip + chips - owner, chips)

        @pl.when((lax.rem(tile, per) == 0) & (lax.rem(far, peers) != place) & (far != 0))
        def _():
            wait_bytes(params.at[pl.ds(0, per)], par_recv.at[owner])

        return tile

    def activate(tile, buf):
        lanes = pl.ds(pl.multiple_of(tile * W, W), W)
        w = params[tile, 0:10]
        rtaps[tile] = dot(params[tile, 10:18].astype(BF16), turn[...], ((1,), (0,)))
        g16, c16 = [], []
        for s in range(3):
            shift[buf, s, 6:8] = tail_in[2 * s : 2 * s + 2, lanes]
        for r in range(0, W, STEP):
            rows = slice(r, r + STEP)
            m1, m2 = tmask[0, rows], tmask[1, rows]
            acts = []
            for s in range(3):
                now = x[s, rows, lanes].astype(F32)
                shift[buf, s, 8 + r : 8 + r + STEP] = now
                acts.append(
                    w[3 * s : 3 * s + 1] * now
                    + w[3 * s + 1 : 3 * s + 2] * (shift[buf, s, 7 + r : 7 + r + STEP] * m1)
                    + w[3 * s + 2 : 3 * s + 3] * (shift[buf, s, 6 + r : 6 + r + STEP] * m2)
                )
                act[s, rows, lanes] = acts[s]
            g16.append((acts[1] * acts[2]).astype(BF16))
            c16.append((cot[rows, lanes].astype(F32) * acts[0]).astype(BF16))
        g_own[tile] = jnp.concatenate(g16, axis=0).T
        c_own[tile] = jnp.concatenate(c16, axis=0).T

    def send_halo(tile):
        remote(g_own.at[tile], g_prev.at[tile], g_send, g_recv.at[tile], nxt).start()
        remote(c_own.at[tile], c_next.at[tile], c_send, c_recv.at[tile], prv).start()

    def forward(i, carry):
        pair = [get_params(2 * i + q) for q in range(2)]
        for q in range(2):
            activate(pair[q], q)
        for q in range(2):
            send_halo(pair[q])
        return carry

    lax.fori_loop(0, tiles // 2, forward, 0)

    shift[:, :, W + 8 : W + 16] = jnp.zeros((2, 3, 8, W), F32)
    lane_group = lax.broadcasted_iota(jnp.int32, (W, W), 1) // 16

    def circulant(row):
        spread = jnp.broadcast_to(row, (W, W))
        return pltpu.roll(spread, 0, 1, stride=1, stride_axis=0).astype(BF16)

    def lanes_of(tile):
        return pl.ds(pl.multiple_of(tile * W, W), W)

    def tile_at(i):
        return lax.rem(chip * per + i, tiles)

    def arrived(tile):
        wait_bytes(g_prev.at[tile], g_recv.at[tile])
        wait_bytes(c_next.at[tile], c_recv.at[tile])

    def convolve(tile, buf):
        lanes = lanes_of(tile)
        taps = params[tile, 10:18]
        flipped = rtaps[tile]
        k_own, k_prev, k_next, o_own, o_next = [bmask[q] for q in range(5)]
        g16 = (act[1, :, lanes] * act[2, :, lanes]).astype(BF16)
        cc = jnp.concatenate([c_own[tile], c_next[tile]], axis=1)
        gg = jnp.concatenate([g_prev[tile], g_own[tile]], axis=1)
        for g in range(8):
            fwd = circulant(taps[g : g + 1])
            rev = circulant(flipped[g : g + 1])
            rows = slice(16 * g, 16 * g + 16)
            weights = jnp.concatenate(
                [
                    jnp.concatenate([fwd * k_prev, fwd * k_own], axis=0),
                    jnp.concatenate([rev * o_own, rev * o_next], axis=0),
                ],
                axis=1,
            )
            both_ways = dot(
                jnp.concatenate([gg[rows], cc[rows]], axis=0), weights, ((1,), (0,))
            )
            sums_t[buf, 0, rows] = both_ways[0:16, :W]
            sums_t[buf, 1, rows] = both_ways[16:32, W:]
            pair = dot(jnp.where(lane_group == g, g16, jnp.zeros_like(g16)), cc, ((1,), (0,)))
            pair = pair.astype(BF16)
            pair = pair[:, :W] * k_own + pair[:, W:] * k_next
            for q in range(8):
                turned[buf, rows, q * W : q * W + W] = pair[16 * q : 16 * q + 16]

    def combine(tile, buf):
        flat[buf, 0] = sums_t[buf, 0].T
        flat[buf, 1] = sums_t[buf, 1].T
        lanes = lanes_of(tile)
        w = params[tile, 0:10]
        gain = w[9:10]
        sums = [jnp.zeros((8, W), F32)] * 10

        def fold(a):
            return jnp.sum(a.reshape(STEP // 8, 8, W), axis=0)

        for r in range(W - STEP, -1, -STEP):
            rows = slice(r, r + STEP)
            q_act, k_act, v_act = act[0, rows, lanes], act[1, rows, lanes], act[2, rows, lanes]
            gated = k_act * v_act
            cotan = cot[rows, lanes].astype(F32)
            cgrad = cotan * q_act
            convolved = flat[buf, 0, rows] + gain * gated
            ggrad = flat[buf, 1, rows] + gain * cgrad
            out[0, rows, lanes] = (q_act * convolved).astype(BF16)
            sums[9] = sums[9] + fold(cgrad * gated)
            u1, u2 = tmask[2, rows], tmask[3, rows]
            for s, ag in enumerate((cotan * convolved, ggrad * v_act, ggrad * k_act)):
                shift[buf, s, 8 + r : 8 + r + STEP] = ag
                b1 = shift[buf, s, 9 + r : 9 + r + STEP] * u1
                b2 = shift[buf, s, 10 + r : 10 + r + STEP] * u2
                sgrad = (
                    w[3 * s : 3 * s + 1] * ag
                    + w[3 * s + 1 : 3 * s + 2] * b1
                    + w[3 * s + 2 : 3 * s + 3] * b2
                )
                out[s + 1, rows, lanes] = sgrad.astype(BF16)
                now = x[s, rows, lanes].astype(F32)
                for k, b in enumerate((ag, b1, b2)):
                    sums[3 * s + k] = sums[3 * s + k] + fold(now * b)
                if r == W - STEP:
                    last[s, :, lanes] = sgrad[STEP - 16 :]
                if r == 0:
                    edge[tile, 2 * s : 2 * s + 2] = ag[0:2]
        for q in range(10):
            total = jnp.sum(sums[q], axis=0, keepdims=True)
            if q < 9 and q % 3 > 0:
                s = q // 3
                head = shift[buf, s, 8:10] * tmask[q % 3 - 1, 0:2]
                before = tail_in[2 * s : 2 * s + 2, lanes]
                if q % 3 == 1:
                    total = total + head[0:1] * before[1:2]
                else:
                    total = total + head[0:1] * before[0:1] + head[1:2] * before[1:2]
            part[tile, q : q + 1] = total
        edge[tile, 6:8] = jnp.zeros((2, W), F32)

    def skew(two):
        diag = dot(turned[...].reshape(2 * W, 8 * W), perm[...], ((1,), (0,)))
        for g in range(16):
            row = pltpu.roll(diag[16 * g : 16 * g + 16], 0, 1, stride=1, stride_axis=0)
            at = 10 + g % 8
            part[two[g // 8], at : at + 1] = jnp.sum(row, axis=0, keepdims=True)

    def send(tile):
        owner = tile // per
        remote(edge.at[tile], edge_in.at[tile], e_send, e_recv, prv).start()

        @pl.when(owner != chip)
        def _():
            slot = part_in.at[lax.rem(tile, per), lax.rem(chip + chips - owner, chips) - 1]
            remote(part.at[tile], slot, r_send, r_recv, owner * CORES + core).start()

    def both(i, carry):
        done = [tile_at(2 * i - 2 + q) for q in range(2)]
        now = [tile_at(2 * i + q) for q in range(2)]
        for q in range(2):
            arrived(now[q])
        skew(done)
        for q in range(2):
            combine(done[q], q)
        for q in range(2):
            convolve(now[q], q)
        for q in range(2):
            send(done[q])
        return carry

    for q in range(2):
        arrived(tile_at(q))
    for q in range(2):
        convolve(tile_at(q), q)
    lax.fori_loop(1, tiles // 2, both, 0)
    skew([tile_at(tiles - 2 + q) for q in range(2)])
    for q in range(2):
        combine(tile_at(tiles - 2 + q), q)
    for q in range(2):
        send(tile_at(tiles - 2 + q))

    wait_bytes(part_in, r_recv)
    for p in range(per):
        total = part[chip * per + p]
        for d in range(chips - 1):
            total = total + part_in[p, d]
        block[p] = total

    def send_block(d, carry):
        to_dp = lax.rem(dp + d // CORES, dps)
        to = chip * CORES + lax.rem(core + d, CORES)
        remote(block, block_in.at[d - 1], b_send, b_recv, to, to_dp).start()
        return carry

    lax.fori_loop(1, CORES * dps, send_block, 0)

    wait_bytes(edge_in, e_recv)
    zero14 = jnp.zeros((14, W), F32)

    def finish(tile, carry):
        lanes = pl.ds(pl.multiple_of(tile * W, W), W)
        w = params[tile, 0:10]
        for s in range(3):
            e0 = edge_in[tile, 2 * s : 2 * s + 1]
            e1 = edge_in[tile, 2 * s + 1 : 2 * s + 2]
            w1, w2 = w[3 * s + 1 : 3 * s + 2], w[3 * s + 2 : 3 * s + 3]
            r0 = w2 * (e0 * tmask[3, W - 2 : W - 1])
            r1 = w1 * (e0 * tmask[2, W - 1 : W]) + w2 * (e1 * tmask[3, W - 1 : W])
            more = jnp.concatenate([zero14, r0, r1], axis=0)
            out[s + 1, W - 16 : W, lanes] = (last[s, :, lanes] + more).astype(BF16)
        return carry

    lax.fori_loop(0, tiles, finish, 0, unroll=2)
    wait_bytes(block_in, b_recv)
    total = block[0]
    for d in range(CORES * dps - 1):
        total = total + block_in[d, 0]
    total = total * scale
    top, low = total[0:10], total[10:18]
    small_out[0:10] = jnp.where(core == 0, top, pltpu.roll(top, W // 2, 1))
    small_out[16:20] = jnp.where(core == 0, low[0:4], low[4:8])
    small_out[20:24] = jnp.zeros((4, W), F32)

    def sent_params(d):
        wait_bytes(params.at[pl.ds(0, per)], par_send.at[d])
        wait_bytes(block_in, par_pass.at[d])

    each_round(sent_params)
    wait_bytes(g_own, g_send)
    wait_bytes(c_own, c_send)
    wait_bytes(edge, e_send)
    wait_bytes(part.at[pl.ds(0, (chips - 1) * per)], r_send)
    wait_bytes(block_in, b_send)


def hand_over(out, small, mixed, grad, short_grad, taps_grad, gain_grad, sem):
    copies = [pltpu.make_async_copy(out.at[0], mixed, sem.at[0])]
    for s in range(3):
        copies.append(pltpu.make_async_copy(out.at[s + 1], grad.at[s], sem.at[s + 1]))
    for copy in copies:
        copy.start()
    for s in range(3):
        short_grad[s] = small[3 * s : 3 * s + 3, : W // 2]
    gain_grad[...] = small[9:10, : W // 2]
    s_at = lax.broadcasted_iota(jnp.int32, (W, W), 0)
    t_at = lax.broadcasted_iota(jnp.int32, (W, W), 1)
    flip = jnp.where(s_at + t_at == W - 1, 1.0, 0.0)
    taps_grad[...] = lax.dot_general(
        small[16:24], flip, (((1,), (0,)), ((), ())),
        precision=lax.Precision.HIGHEST, preferred_element_type=F32,
    )[0:4]
    for copy in copies:
        copy.wait()


def local(streams, cotangent, doc_ids, short_taps, long_taps, skip_gain):
    channels = cotangent.shape[2]
    n, dps = lax.axis_size("seq"), lax.axis_size("dp")
    tiles, chips = channels // W, n // CORES
    per = tiles // chips
    x = jnp.transpose(streams[0], (1, 0, 2))
    scale = 1.0 / math.sqrt(dps * n * W)
    dma, vmem = pltpu.SemaphoreType.DMA, pltpu.VMEM
    any_, inv = pl.BlockSpec(memory_space=pltpu.HBM), pl.BlockSpec(memory_space=pltpu.VMEM)
    out, small = pl.pallas_call(
        functools.partial(kernel, tiles, chips, dps, scale),
        out_shape=(
            jax.ShapeDtypeStruct((4, W, channels), BF16),
            jax.ShapeDtypeStruct((24, W), F32),
        ),
        in_specs=[any_] * 6,
        out_specs=(inv, inv),
        scratch_shapes=[
            vmem((3, W, channels), BF16),
            vmem((W, channels), BF16),
            vmem(doc_ids.shape, jnp.int32),
            vmem(short_taps.shape, F32),
            vmem(long_taps.shape, F32),
            vmem((1,) + skip_gain.shape, F32),
            vmem((3, W, channels), F32),
            vmem((tiles, W, W), BF16),
            vmem((tiles, W, W), BF16),
            vmem((tiles, W, W), BF16),
            vmem((tiles, W, W), BF16),
            vmem((per, PR, W), F32),
            vmem((per, PR, W), F32),
            vmem((tiles, PR, W), F32),
            vmem((8, channels), F32),
            vmem((8, channels), F32),
            vmem((1, W), jnp.int32),
            vmem((1, W), jnp.int32),
            vmem((tiles, 8, W), F32),
            vmem((tiles, 8, W), F32),
            vmem((3, 16, channels), F32),
            vmem((tiles, PR, W), F32),
            vmem((per, chips - 1, PR, W), F32),
            vmem((per, PR, W), F32),
            vmem((CORES * dps - 1, per, PR, W), F32),
            vmem((5, W, W), BF16),
            vmem((8 * W, W), BF16),
            vmem((W, W), BF16),
            vmem((tiles, 8, W), F32),
            vmem((4, W, W), F32),
            vmem((W + 16, W), F32),
            vmem((2, 3, W + 16, W), F32),
            vmem((2, 2, W, W), F32),
            vmem((2, W, 8 * W), BF16),
            vmem((2, 2, W, W), F32),
            dma((6,)),
            dma((2,)),
            dma((chips,)),
            dma((chips,)),
            dma((chips,)),
            dma((2,)),
            dma((4,)),
            dma(()),
            dma((tiles,)),
            dma(()),
            dma((tiles,)),
            dma(()),
            dma(()),
            dma(()),
            dma(()),
            dma(()),
            dma(()),
        ],
        compiler_params=pltpu.CompilerParams(
            collective_id=0, has_side_effects=True, vmem_limit_bytes=32 * 1024 * 1024
        ),
        cost_estimate=pl.CostEstimate(
            flops=6 * W * W * channels, bytes_accessed=16 * W * channels, transcendentals=0
        ),
        name="hyena_block",
    )(
        *(
            pltpu.with_memory_space_constraint(a, pltpu.HBM)
            for a in (x, cotangent[0], doc_ids, short_taps, long_taps, skip_gain.reshape(1, -1))
        )
    )
    mixed, grad, short_grad, taps_grad, gain_grad = pl.pallas_call(
        hand_over,
        out_shape=(
            jax.ShapeDtypeStruct((W, channels), BF16),
            jax.ShapeDtypeStruct((3, W, channels), BF16),
            jax.ShapeDtypeStruct((3, 3, W // 2), F32),
            jax.ShapeDtypeStruct((4, W), F32),
            jax.ShapeDtypeStruct((1, W // 2), F32),
        ),
        in_specs=[inv, inv],
        out_specs=(any_, any_, inv, inv, inv),
        scratch_shapes=[dma((4,))],
        compiler_params=pltpu.CompilerParams(vmem_limit_bytes=16 * 1024 * 1024),
        name="hand_over",
    )(out, small)
    return (
        mixed[None],
        jnp.transpose(grad, (1, 0, 2))[None],
        short_grad,
        taps_grad,
        gain_grad.reshape(W // 2),
    )


def solution(mesh):
    return jax.shard_map(
        local,
        mesh=mesh,
        in_specs=(
            P("dp", "seq", None, None),
            P("dp", "seq", None),
            P("dp", "seq"),
            P(None, None, "seq"),
            P("seq", None),
            P("seq"),
        ),
        out_specs=(
            P("dp", "seq", None),
            P("dp", "seq", None, None),
            P(None, None, "seq"),
            P("seq", None),
            P("seq"),
        ),
        check_vma=False,
    )
```

```python
import functools
import math

import jax
import jax.numpy as jnp
from jax import lax
from jax.experimental import pallas as pl
from jax.experimental.pallas import tpu as pltpu
from jax.sharding import PartitionSpec as P

F32 = jnp.float32
BF16 = jnp.bfloat16
W = 128
PR = 18
CORES = 2
STEP = 32


def dot(a, b, dims):
    return lax.dot_general(a, b, (dims, ((), ())), preferred_element_type=F32)


def kernel(
    tiles, chips, dps, scale,
    x_hbm, cot_hbm, ids_hbm, short_hbm, taps_hbm, gain_hbm,
    out, small_out,
    x, cot, ids_ref, short_ref, taps_ref, gain_ref, act, g_own, c_own, g_prev, c_next,
    half, half_in, params, tail, tail_in, idp, idn, edge, edge_in, last,
    part, part_in, block, block_in,
    bmask, perm, turn, rtaps, tmask, idx, shift, sums_t, turned, flat,
    load_sem, half_sem, par_send, par_pass, par_recv, tail_sem, id_sem,
    g_send, g_recv, c_send, c_recv, e_send, e_recv, r_send, r_recv, b_send, b_recv,
):
    per = tiles // chips
    seq = lax.axis_index("seq")
    dp = lax.axis_index("dp")
    chip, core = seq // CORES, lax.rem(seq, CORES)
    n = chips * CORES
    nxt, prv = lax.rem(seq + 1, n), lax.rem(seq + n - 1, n)
    sib = chip * CORES + 1 - core

    def remote(src, dst, send, recv, to, to_dp=None):
        where = {"seq": to} if to_dp is None else {"dp": to_dp, "seq": to}
        return pltpu.make_async_remote_copy(
            src_ref=src, dst_ref=dst, send_sem=send, recv_sem=recv,
            device_id=where, device_id_type=pl.DeviceIdType.MESH,
        )

    def wait_bytes(ref, sem):
        pltpu.make_async_copy(ref, ref, sem).wait()

    load_x = pltpu.make_async_copy(x_hbm, x, load_sem.at[0])
    load_c = pltpu.make_async_copy(cot_hbm, cot, load_sem.at[1])
    small = [
        pltpu.make_async_copy(a, b, load_sem.at[2 + q])
        for q, (a, b) in enumerate(
            ((ids_hbm, ids_ref), (short_hbm, short_ref), (taps_hbm, taps_ref), (gain_hbm, gain_ref))
        )
    ]
    for copy in small:
        copy.start()
    load_x.start()
    load_c.start()
    peers = dps * CORES
    place = dp * CORES + core

    barrier = pltpu.get_barrier_semaphore()

    def greet(to, to_dp=None):
        where = {"seq": to} if to_dp is None else {"dp": to_dp, "seq": to}
        pl.semaphore_signal(barrier, 1, device_id=where, device_id_type=pl.DeviceIdType.MESH)

    greet(nxt)
    greet(prv)
    greet(sib)

    def greet_chip(d, carry):
        greet(lax.rem(chip + d, chips) * CORES + core)
        return carry

    lax.fori_loop(1, chips, greet_chip, 0)

    def greet_dp(d, carry):
        other = lax.rem(dp + d, dps)
        greet(seq, other)
        greet(sib, other)
        return carry

    lax.fori_loop(1, dps, greet_dp, 0)
    pl.semaphore_wait(barrier, 3 + (chips - 1) + 2 * (dps - 1))

    for copy in small:
        copy.wait()
    id_to_next = remote(ids_ref, idp, id_sem.at[0], id_sem.at[1], nxt)
    id_to_prev = remote(ids_ref, idn, id_sem.at[2], id_sem.at[3], prv)
    id_to_next.start()
    id_to_prev.start()
    lane = lax.broadcasted_iota(jnp.int32, (10, W), 1)
    row = lax.broadcasted_iota(jnp.int32, (8, W), 0)
    sg = jnp.concatenate([short_ref[0], short_ref[1], short_ref[2], gain_ref[...]], axis=0)[:, : W // 2]
    sg = jnp.where(lane // (W // 2) == core, jnp.concatenate([sg, sg], axis=1), 0.0)
    tp = taps_ref[0:4]
    tp = jnp.where(row // 4 == core, jnp.concatenate([tp, tp], axis=0), 0.0)
    for p in range(per):
        half[p, 0:10] = sg
        half[p, 10:18] = tp
    to_sib = remote(half, half_in, half_sem.at[0], half_sem.at[1], sib)
    to_sib.start()

    load_x.wait()
    for i in range(3):
        rows = x[i, W - 16 : W].astype(F32)
        tail[2 * i : 2 * i + 2] = rows[14:16]
    tail[6:8] = jnp.zeros((2, tiles * W), F32)
    tail_to_next = remote(tail, tail_in, tail_sem.at[0], tail_sem.at[1], nxt)
    tail_to_next.start()

    to_sib.wait()
    params[pl.ds(chip * per, per)] = half[...] + half_in[...]

    rounds = -(-chips // peers)

    def each_round(act_on):
        def body(m, carry):
            d = place + peers * m

            @pl.when((d > 0) & (d < chips))
            def _():
                act_on(d)

            return carry

        lax.fori_loop(0, rounds, body, 0)

    def send_params(d):
        mine = params.at[pl.ds(chip * per, per)]
        to = lax.rem(chip + chips - d, chips) * CORES + core
        remote(mine, mine, par_send.at[d], par_recv.at[chip], to).start()

    def pass_params(d):
        source = lax.rem(chip + d, chips)
        mine = params.at[pl.ds(source * per, per)]
        wait_bytes(mine, par_recv.at[source])

        def one(e, carry):
            peer = lax.rem(place + e, peers)
            to = chip * CORES + lax.rem(peer, CORES)
            remote(mine, mine, par_pass.at[d], par_recv.at[source], to, peer // CORES).start()
            return carry

        lax.fori_loop(1, peers, one, 0)

    each_round(send_params)

    id_to_next.wait()
    id_to_prev.wait()
    own_row = jnp.broadcast_to(ids_ref[...], (W, W)).astype(F32)
    prev_row = jnp.broadcast_to(jnp.where(seq == 0, -1, idp[...]), (W, W)).astype(F32)
    next_row = jnp.broadcast_to(jnp.where(seq == n - 1, -2, idn[...]), (W, W)).astype(F32)
    own_col, prev_col, next_col = own_row.T, prev_row.T, next_row.T
    s_at = lax.broadcasted_iota(jnp.int32, (W, W), 0)
    t_at = lax.broadcasted_iota(jnp.int32, (W, W), 1)
    same_own = jnp.where((s_at <= t_at) & (own_col == own_row), 1.0, 0.0)
    same_prev = jnp.where((s_at > t_at) & (prev_col == own_row), 1.0, 0.0)
    same_next = jnp.where((s_at > t_at) & (own_col == next_row), 1.0, 0.0)
    bmask[0] = same_own.astype(BF16)
    bmask[1] = same_prev.astype(BF16)
    bmask[2] = same_next.astype(BF16)
    bmask[3] = same_own.T.astype(BF16)
    bmask[4] = same_next.T.astype(BF16)
    turn[...] = jnp.where((s_at + t_at) % W == 0, 1.0, 0.0).astype(BF16)
    for q in range(8):
        perm[q * W : q * W + W] = jnp.where(
            (s_at + t_at + 1 - 16 * q) % W == 0, 1.0, 0.0
        ).astype(BF16)
    idx[0:8] = prev_col[W - 8 : W]
    idx[8 : W + 8] = own_col
    idx[W + 8 : W + 16] = next_col[0:8]
    mine = idx[8 : W + 8]
    tmask[0] = jnp.where(idx[7 : W + 7] == mine, 1.0, 0.0)
    tmask[1] = jnp.where(idx[6 : W + 6] == mine, 1.0, 0.0)
    tmask[2] = jnp.where(idx[9 : W + 9] == mine, 1.0, 0.0)
    tmask[3] = jnp.where(idx[10 : W + 10] == mine, 1.0, 0.0)
    each_round(pass_params)
    load_c.wait()
    tail_to_next.wait()

    def get_params(i):
        tile = lax.rem(chip * per + i, tiles)
        owner = tile // per

        far = lax.rem(owner + chips - chip, chips)

        @pl.when((lax.rem(tile, per) == 0) & (lax.rem(far, peers) != place) & (far != 0))
        def _():
            wait_bytes(params.at[pl.ds(0, per)], par_recv.at[owner])

        return tile

    def activate(tile, buf):
        lanes = pl.ds(pl.multiple_of(tile * W, W), W)
        w = params[tile, 0:10]
        rtaps[tile] = dot(params[tile, 10:18].astype(BF16), turn[...], ((1,), (0,)))
        g16, c16 = [], []
        for s in range(3):
            shift[buf, s, 6:8] = tail_in[2 * s : 2 * s + 2, lanes]
        for r in range(0, W, STEP):
            rows = slice(r, r + STEP)
            m1, m2 = tmask[0, rows], tmask[1, rows]
            acts = []
            for s in range(3):
                now = x[s, rows, lanes].astype(F32)
                shift[buf, s, 8 + r : 8 + r + STEP] = now
                acts.append(
                    w[3 * s : 3 * s + 1] * now
                    + w[3 * s + 1 : 3 * s + 2] * (shift[buf, s, 7 + r : 7 + r + STEP] * m1)
                    + w[3 * s + 2 : 3 * s + 3] * (shift[buf, s, 6 + r : 6 + r + STEP] * m2)
                )
                act[s, rows, lanes] = acts[s]
            g16.append((acts[1] * acts[2]).astype(BF16))
            c16.append((cot[rows, lanes].astype(F32) * acts[0]).astype(BF16))
        g_own[tile] = jnp.concatenate(g16, axis=0).T
        c_own[tile] = jnp.concatenate(c16, axis=0).T

    def send_halo(tile):
        remote(g_own.at[tile], g_prev.at[tile], g_send, g_recv.at[tile], nxt).start()
        remote(c_own.at[tile], c_next.at[tile], c_send, c_recv.at[tile], prv).start()

    def forward(i, carry):
        pair = [get_params(2 * i + q) for q in range(2)]
        for q in range(2):
            activate(pair[q], q)
        for q in range(2):
            send_halo(pair[q])
        return carry

    lax.fori_loop(0, tiles // 2, forward, 0)

    shift[:, :, W + 8 : W + 16] = jnp.zeros((2, 3, 8, W), F32)
    lane_group = lax.broadcasted_iota(jnp.int32, (W, W), 1) // 16

    def circulant(row):
        spread = jnp.broadcast_to(row, (W, W))
        return pltpu.roll(spread, 0, 1, stride=1, stride_axis=0).astype(BF16)

    def lanes_of(tile):
        return pl.ds(pl.multiple_of(tile * W, W), W)

    def tile_at(i):
        return lax.rem((chip + 1) * per + i, tiles)

    def arrived(tile):
        wait_bytes(g_prev.at[tile], g_recv.at[tile])
        wait_bytes(c_next.at[tile], c_recv.at[tile])

    def convolve(tile, buf):
        lanes = lanes_of(tile)
        taps = params[tile, 10:18]
        flipped = rtaps[tile]
        k_own, k_prev, k_next, o_own, o_next = [bmask[q] for q in range(5)]
        g16 = (act[1, :, lanes] * act[2, :, lanes]).astype(BF16)
        cc = jnp.concatenate([c_own[tile], c_next[tile]], axis=1)
        gg = jnp.concatenate([g_prev[tile], g_own[tile]], axis=1)
        for g in range(8):
            fwd = circulant(taps[g : g + 1])
            rev = circulant(flipped[g : g + 1])
            rows = slice(16 * g, 16 * g + 16)
            weights = jnp.concatenate(
                [
                    jnp.concatenate([fwd * k_prev, fwd * k_own], axis=0),
                    jnp.concatenate([rev * o_own, rev * o_next], axis=0),
                ],
                axis=1,
            )
            both_ways = dot(
                jnp.concatenate([gg[rows], cc[rows]], axis=0), weights, ((1,), (0,))
            )
            sums_t[buf, 0, rows] = both_ways[0:16, :W]
            sums_t[buf, 1, rows] = both_ways[16:32, W:]
            pair = dot(jnp.where(lane_group == g, g16, jnp.zeros_like(g16)), cc, ((1,), (0,)))
            pair = pair.astype(BF16)
            pair = pair[:, :W] * k_own + pair[:, W:] * k_next
            for q in range(8):
                turned[buf, rows, q * W : q * W + W] = pair[16 * q : 16 * q + 16]

    def combine(tile, buf):
        flat[buf, 0] = sums_t[buf, 0].T
        flat[buf, 1] = sums_t[buf, 1].T
        lanes = lanes_of(tile)
        w = params[tile, 0:10]
        gain = w[9:10]
        sums = [jnp.zeros((8, W), F32)] * 10

        def fold(a):
            return jnp.sum(a.reshape(STEP // 8, 8, W), axis=0)

        for r in range(W - STEP, -1, -STEP):
            rows = slice(r, r + STEP)
            q_act, k_act, v_act = act[0, rows, lanes], act[1, rows, lanes], act[2, rows, lanes]
            gated = k_act * v_act
            cotan = cot[rows, lanes].astype(F32)
            cgrad = cotan * q_act
            convolved = flat[buf, 0, rows] + gain * gated
            ggrad = flat[buf, 1, rows] + gain * cgrad
            out[0, rows, lanes] = (q_act * convolved).astype(BF16)
            sums[9] = sums[9] + fold(cgrad * gated)
            u1, u2 = tmask[2, rows], tmask[3, rows]
            for s, ag in enumerate((cotan * convolved, ggrad * v_act, ggrad * k_act)):
                shift[buf, s, 8 + r : 8 + r + STEP] = ag
                b1 = shift[buf, s, 9 + r : 9 + r + STEP] * u1
                b2 = shift[buf, s, 10 + r : 10 + r + STEP] * u2
                sgrad = (
                    w[3 * s : 3 * s + 1] * ag
                    + w[3 * s + 1 : 3 * s + 2] * b1
                    + w[3 * s + 2 : 3 * s + 3] * b2
                )
                out[s + 1, rows, lanes] = sgrad.astype(BF16)
                now = x[s, rows, lanes].astype(F32)
                for k, b in enumerate((ag, b1, b2)):
                    sums[3 * s + k] = sums[3 * s + k] + fold(now * b)
                if r == W - STEP:
                    last[s, :, lanes] = sgrad[STEP - 16 :]
                if r == 0:
                    edge[tile, 2 * s : 2 * s + 2] = ag[0:2]
        for q in range(10):
            total = jnp.sum(sums[q], axis=0, keepdims=True)
            if q < 9 and q % 3 > 0:
                s = q // 3
                head = shift[buf, s, 8:10] * tmask[q % 3 - 1, 0:2]
                before = tail_in[2 * s : 2 * s + 2, lanes]
                if q % 3 == 1:
                    total = total + head[0:1] * before[1:2]
                else:
                    total = total + head[0:1] * before[0:1] + head[1:2] * before[1:2]
            part[tile, q : q + 1] = total
        edge[tile, 6:8] = jnp.zeros((2, W), F32)

    def skew(two):
        diag = dot(turned[...].reshape(2 * W, 8 * W), perm[...], ((1,), (0,)))
        for g in range(16):
            row = pltpu.roll(diag[16 * g : 16 * g + 16], 0, 1, stride=1, stride_axis=0)
            at = 10 + g % 8
            part[two[g // 8], at : at + 1] = jnp.sum(row, axis=0, keepdims=True)

    def send(tile):
        owner = tile // per
        remote(edge.at[tile], edge_in.at[tile], e_send, e_recv, prv).start()

        @pl.when(owner != chip)
        def _():
            slot = part_in.at[lax.rem(tile, per), lax.rem(chip + chips - owner, chips) - 1]
            remote(part.at[tile], slot, r_send, r_recv, owner * CORES + core).start()

    def both(i, carry):
        done = [tile_at(2 * i - 2 + q) for q in range(2)]
        now = [tile_at(2 * i + q) for q in range(2)]
        for q in range(2):
            arrived(now[q])
        skew(done)
        for q in range(2):
            combine(done[q], q)
        for q in range(2):
            convolve(now[q], q)
        for q in range(2):
            send(done[q])
        return carry

    for q in range(2):
        arrived(tile_at(q))
    for q in range(2):
        convolve(tile_at(q), q)
    lax.fori_loop(1, tiles // 2, both, 0)
    skew([tile_at(tiles - 2 + q) for q in range(2)])
    for q in range(2):
        combine(tile_at(tiles - 2 + q), q)
    for q in range(2):
        send(tile_at(tiles - 2 + q))

    wait_bytes(part_in, r_recv)
    for p in range(per):
        total = part[chip * per + p]
        for d in range(chips - 1):
            total = total + part_in[p, d]
        block[p] = total

    def send_block(d, carry):
        to_dp = lax.rem(dp + d // CORES, dps)
        to = chip * CORES + lax.rem(core + d, CORES)
        remote(block, block_in.at[d - 1], b_send, b_recv, to, to_dp).start()
        return carry

    lax.fori_loop(1, CORES * dps, send_block, 0)

    wait_bytes(edge_in, e_recv)
    zero14 = jnp.zeros((14, W), F32)

    def finish(tile, carry):
        lanes = pl.ds(pl.multiple_of(tile * W, W), W)
        w = params[tile, 0:10]
        for s in range(3):
            e0 = edge_in[tile, 2 * s : 2 * s + 1]
            e1 = edge_in[tile, 2 * s + 1 : 2 * s + 2]
            w1, w2 = w[3 * s + 1 : 3 * s + 2], w[3 * s + 2 : 3 * s + 3]
            r0 = w2 * (e0 * tmask[3, W - 2 : W - 1])
            r1 = w1 * (e0 * tmask[2, W - 1 : W]) + w2 * (e1 * tmask[3, W - 1 : W])
            more = jnp.concatenate([zero14, r0, r1], axis=0)
            out[s + 1, W - 16 : W, lanes] = (last[s, :, lanes] + more).astype(BF16)
        return carry

    lax.fori_loop(0, tiles, finish, 0, unroll=2)
    wait_bytes(block_in, b_recv)
    total = block[0]
    for d in range(CORES * dps - 1):
        total = total + block_in[d, 0]
    total = total * scale
    top, low = total[0:10], total[10:18]
    small_out[0:10] = jnp.where(core == 0, top, pltpu.roll(top, W // 2, 1))
    small_out[16:20] = jnp.where(core == 0, low[0:4], low[4:8])
    small_out[20:24] = jnp.zeros((4, W), F32)

    def sent_params(d):
        wait_bytes(params.at[pl.ds(0, per)], par_send.at[d])
        wait_bytes(block_in, par_pass.at[d])

    each_round(sent_params)
    wait_bytes(g_own, g_send)
    wait_bytes(c_own, c_send)
    wait_bytes(edge, e_send)
    wait_bytes(part.at[pl.ds(0, (chips - 1) * per)], r_send)
    wait_bytes(block_in, b_send)


def hand_over(out, small, mixed, grad, short_grad, taps_grad, gain_grad, sem):
    copies = [pltpu.make_async_copy(out.at[0], mixed, sem.at[0])]
    for s in range(3):
        copies.append(pltpu.make_async_copy(out.at[s + 1], grad.at[s], sem.at[s + 1]))
    for copy in copies:
        copy.start()
    for s in range(3):
        short_grad[s] = small[3 * s : 3 * s + 3, : W // 2]
    gain_grad[...] = small[9:10, : W // 2]
    s_at = lax.broadcasted_iota(jnp.int32, (W, W), 0)
    t_at = lax.broadcasted_iota(jnp.int32, (W, W), 1)
    flip = jnp.where(s_at + t_at == W - 1, 1.0, 0.0)
    taps_grad[...] = lax.dot_general(
        small[16:24], flip, (((1,), (0,)), ((), ())),
        precision=lax.Precision.HIGHEST, preferred_element_type=F32,
    )[0:4]
    for copy in copies:
        copy.wait()


def local(streams, cotangent, doc_ids, short_taps, long_taps, skip_gain):
    channels = cotangent.shape[2]
    n, dps = lax.axis_size("seq"), lax.axis_size("dp")
    tiles, chips = channels // W, n // CORES
    per = tiles // chips
    x = jnp.transpose(streams[0], (1, 0, 2))
    scale = 1.0 / math.sqrt(dps * n * W)
    dma, vmem = pltpu.SemaphoreType.DMA, pltpu.VMEM
    any_, inv = pl.BlockSpec(memory_space=pltpu.HBM), pl.BlockSpec(memory_space=pltpu.VMEM)
    out, small = pl.pallas_call(
        functools.partial(kernel, tiles, chips, dps, scale),
        out_shape=(
            jax.ShapeDtypeStruct((4, W, channels), BF16),
            jax.ShapeDtypeStruct((24, W), F32),
        ),
        in_specs=[any_] * 6,
        out_specs=(inv, inv),
        scratch_shapes=[
            vmem((3, W, channels), BF16),
            vmem((W, channels), BF16),
            vmem(doc_ids.shape, jnp.int32),
            vmem(short_taps.shape, F32),
            vmem(long_taps.shape, F32),
            vmem((1,) + skip_gain.shape, F32),
            vmem((3, W, channels), F32),
            vmem((tiles, W, W), BF16),
            vmem((tiles, W, W), BF16),
            vmem((tiles, W, W), BF16),
            vmem((tiles, W, W), BF16),
            vmem((per, PR, W), F32),
            vmem((per, PR, W), F32),
            vmem((tiles, PR, W), F32),
            vmem((8, channels), F32),
            vmem((8, channels), F32),
            vmem((1, W), jnp.int32),
            vmem((1, W), jnp.int32),
            vmem((tiles, 8, W), F32),
            vmem((tiles, 8, W), F32),
            vmem((3, 16, channels), F32),
            vmem((tiles, PR, W), F32),
            vmem((per, chips - 1, PR, W), F32),
            vmem((per, PR, W), F32),
            vmem((CORES * dps - 1, per, PR, W), F32),
            vmem((5, W, W), BF16),
            vmem((8 * W, W), BF16),
            vmem((W, W), BF16),
            vmem((tiles, 8, W), F32),
            vmem((4, W, W), F32),
            vmem((W + 16, W), F32),
            vmem((2, 3, W + 16, W), F32),
            vmem((2, 2, W, W), F32),
            vmem((2, W, 8 * W), BF16),
            vmem((2, 2, W, W), F32),
            dma((6,)),
            dma((2,)),
            dma((chips,)),
            dma((chips,)),
            dma((chips,)),
            dma((2,)),
            dma((4,)),
            dma(()),
            dma((tiles,)),
            dma(()),
            dma((tiles,)),
            dma(()),
            dma(()),
            dma(()),
            dma(()),
            dma(()),
            dma(()),
        ],
        compiler_params=pltpu.CompilerParams(
            collective_id=0, has_side_effects=True, vmem_limit_bytes=32 * 1024 * 1024
        ),
        cost_estimate=pl.CostEstimate(
            flops=6 * W * W * channels, bytes_accessed=16 * W * channels, transcendentals=0
        ),
        name="hyena_block",
    )(
        *(
            pltpu.with_memory_space_constraint(a, pltpu.HBM)
            for a in (x, cotangent[0], doc_ids, short_taps, long_taps, skip_gain.reshape(1, -1))
        )
    )
    mixed, grad, short_grad, taps_grad, gain_grad = pl.pallas_call(
        hand_over,
        out_shape=(
            jax.ShapeDtypeStruct((W, channels), BF16),
            jax.ShapeDtypeStruct((3, W, channels), BF16),
            jax.ShapeDtypeStruct((3, 3, W // 2), F32),
            jax.ShapeDtypeStruct((4, W), F32),
            jax.ShapeDtypeStruct((1, W // 2), F32),
        ),
        in_specs=[inv, inv],
        out_specs=(any_, any_, inv, inv, inv),
        scratch_shapes=[dma((4,))],
        compiler_params=pltpu.CompilerParams(vmem_limit_bytes=16 * 1024 * 1024),
        name="hand_over",
    )(out, small)
    return (
        mixed[None],
        jnp.transpose(grad, (1, 0, 2))[None],
        short_grad,
        taps_grad,
        gain_grad.reshape(W // 2),
    )


def solution(mesh):
    return jax.shard_map(
        local,
        mesh=mesh,
        in_specs=(
            P("dp", "seq", None, None),
            P("dp", "seq", None),
            P("dp", "seq"),
            P(None, None, "seq"),
            P("seq", None),
            P("seq"),
        ),
        out_specs=(
            P("dp", "seq", None),
            P("dp", "seq", None, None),
            P(None, None, "seq"),
            P("seq", None),
            P("seq"),
        ),
        check_vma=False,
    )
```
